256 devices in a mesh: va: 8 (over x, y_hi), vb: 8 (over z), occ: 4 (over y_lo, core).
Axes of the slice: x: 4, y: 4 (y_hi: 2, y_lo: 2; y = y_hi * 2 + y_lo), z: 8, core: 2. Of those that a mesh axis runs over, the one named last changes fastest.
Arguments:
- amplitudes: bfloat16 [768, 800, 800], P(('va', 'vb', 'occ')), may hold values from -6 to 6
- integrals: bfloat16 [800, 800, 1024], P('va', ('vb', 'occ')), may hold values from -0.01953125 to 0.01953125
- virt_irrep: int32 [800], replicated, may hold values from 0 to 7
- slab_irrep: int32 [1024], replicated, may hold values from 0 to 7
Outputs:
- ladder: float32 [768, 1024], P(('va', 'vb', 'occ'))
The draws below stay inside these ranges and needn't reach their ends.
Inputs may be any that keep to these rules, and one draw needn't show every extreme that they name: `virt_irrep`: irrep labels of the D2h group. `slab_irrep`: irrep labels of the D2h group.
All inputs are finite; a program needn't handle non-finite values.
Results may differ from the reference program's by a relative error of at most 0.0003.
Values may be sent and summed in bfloat16 or wider, within the bound.
No kernel may reach another device: no remote copies, remote signals or barrier semaphores. Data moves between devices by JAX's collectives and lax.ppermute only.
A program may use at most 128 MiB of HBM per device.

```python
import math
import jax
import jax.numpy as jnp
from jax import lax

V = 800
SLAB = 1024
NP = 768


def set_ends(array, rng, least, largest):
    longest = array.shape.index(max(array.shape))
    spots = []
    for shift in (0, 1):
        where = [jax.random.randint(jax.random.fold_in(rng, axis), (), 0, length) for axis, length in enumerate(array.shape)]
        where[longest] = (where[longest] + shift) % array.shape[longest]
        spots.append(tuple(where))
    return array.at[spots[0]].set(least).at[spots[1]].set(largest)


def levels(rng, extent, cuts, smallest, largest):
    gain = 1.0
    for position, parts in cuts:
        heights = jax.random.uniform(jax.random.fold_in(jax.random.fold_in(rng, 6), position), (parts,), jnp.float32, smallest / len(cuts), largest / len(cuts))
        gain = gain * jnp.repeat(jnp.exp(heights), extent[position] // parts).reshape((-1,) + (1,) * (len(extent) - 1 - position))
    return gain


def bell_draw(own_key, shape, scale, most, pieces=(), held_as=jnp.bfloat16):
    values = scale * jax.random.normal(own_key, shape, jnp.float32)
    if pieces:
        values = values * levels(own_key, shape, pieces, -0.22, 0.18)
    return jnp.clip(values, -most, most).astype(held_as)


def setup_inputs(seed: int = 0) -> dict:
    key_of = jax.random.split(jax.random.key(seed), 5)
    amplitudes = bell_draw(key_of[0], (NP, V, V), 1.0, 6.0, ((0, 256),))
    integrals = bell_draw(key_of[1], (V, V, SLAB), (V * V // 8) ** -0.5, 0.01953125, ((0, 8), (1, 32)))
    virt_irrep = set_ends(jax.random.randint(key_of[2], (V,), 0, 8), jax.random.fold_in(key_of[2], 1), 0, 7).astype(jnp.int32)
    slab_irrep = set_ends(jax.random.randint(key_of[3], (SLAB,), 0, 8), jax.random.fold_in(key_of[3], 1), 0, 7).astype(jnp.int32)
    return {"amplitudes": amplitudes, "integrals": integrals, "virt_irrep": virt_irrep, "slab_irrep": slab_irrep}


def reference(amplitudes, integrals, virt_irrep, slab_irrep):
    width = math.gcd(V, 32)
    count = V // width

    def step(k, total):
        start = (k * width).astype(jnp.int32)
        rows = lax.dynamic_slice_in_dim(integrals, start, width, 0)
        labels = lax.dynamic_slice_in_dim(virt_irrep, start, width, 0)
        allowed = jnp.bitwise_xor(labels[:, None, None], virt_irrep[None, :, None]) == slab_irrep[None, None, :]
        masked = jnp.where(allowed, rows, jnp.zeros_like(rows))
        block = lax.dynamic_slice_in_dim(amplitudes, start, width, 1)
        return total + jnp.dot(block.reshape(NP, width * V), masked.reshape(width * V, SLAB), preferred_element_type=jnp.float32)

    return lax.fori_loop(0, count, step, jnp.zeros((NP, SLAB), jnp.float32))
```

```python
import functools

import jax
import jax.numpy as jnp
from jax import lax
from jax.experimental import pallas as pl
from jax.experimental.pallas import tpu as pltpu
from jax.sharding import PartitionSpec as P

LANES = 128
IRREPS = 8
SPARE = 32
CAP = LANES + SPARE
QUARTERS = LANES // SPARE
VMEM_LIMIT = 56 * 1024 * 1024
SOURCES = ("occ", "va")


def iota(shape, axis):
    return lax.broadcasted_iota(jnp.int32, shape, axis)


def one_hot(hits):
    return jnp.where(hits, 1.0, 0.0).astype(jnp.bfloat16)


def dot(a, b):
    return jnp.dot(a, b, preferred_element_type=jnp.float32)


def pack_kernel(
    folds, round_ref, second_ref, block_ref, first_ref, row_ref, col_ref,
    packed_ref, rank_ref, onehot, main, over, stage_main, stage_over,
):
    step = pl.program_id(0)
    per_step, first_width, slab = block_ref.shape
    second_width = per_step * pl.num_programs(0)
    pitch = main.shape[0] // second_width
    groups = first_width // folds
    chunk = LANES
    row = row_ref[...]

    @pl.when(step == 0)
    def _():
        base = round_ref[0] * CAP

        def ranks(k, total):
            start = pl.multiple_of(k * chunk, chunk)
            same = col_ref[pl.ds(start, chunk), :] == row
            own = iota((chunk, slab), 0) + start
            other = iota((chunk, slab), 1)
            rank = jnp.sum(jnp.where(same & (other < own), 1.0, 0.0), axis=1, keepdims=True)
            lane = iota((chunk, 2 * LANES), 1).astype(jnp.float32)
            onehot[pl.ds(start, chunk), :] = one_hot(lane == rank - base.astype(jnp.float32))
            return total + jnp.sum(jnp.where(same & (own < other), 1.0, 0.0), axis=0, keepdims=True)

        total = lax.fori_loop(0, slab // chunk, ranks, jnp.zeros((1, slab), jnp.float32))
        rank_ref[...] = total.astype(jnp.int32)

    for k in range(per_step):
        d = step * per_step + k
        allowed = jnp.bitwise_xor(first_ref[...], second_ref[d]) == row
        masked = jnp.where(allowed, block_ref[k].astype(jnp.float32), 0.0).astype(jnp.bfloat16)
        packed = dot(masked, onehot[...])
        start = pl.multiple_of(d * pitch, 8)
        main[pl.ds(start, first_width), :] = packed[:, :LANES]
        over[pl.ds(start, first_width), :] = packed[:, LANES:]

    @pl.when(step == pl.num_programs(0) - 1)
    def _():
        stage_main[...] = jnp.zeros_like(stage_main)
        stage_over[...] = jnp.zeros_like(stage_over)
        per_quarter = groups // QUARTERS
        low = iota((LANES, LANES), 1) < SPARE

        def assemble(e, carry):
            spare = jnp.zeros((LANES, LANES), jnp.float32)
            for q in range(QUARTERS):
                group = q * per_quarter + e
                for f in range(folds):
                    rows = pl.ds(group * folds + f, second_width, stride=pitch)
                    stage_main[pl.ds(f * second_width, second_width), :] = main[rows, :]
                    stage_over[pl.ds(f * second_width, second_width), :] = over[rows, :]
                at = pl.multiple_of(group * LANES, LANES)
                packed_ref[pl.ds(at, LANES), :] = stage_main[...].astype(jnp.bfloat16)
                piece = jnp.where(low, stage_over[...], 0.0)
                spare = spare + (piece if q == 0 else pltpu.roll(piece, q * SPARE, 1))
            at = pl.multiple_of((groups + e) * LANES, LANES)
            packed_ref[pl.ds(at, LANES), :] = spare.astype(jnp.bfloat16)
            return carry

        lax.fori_loop(0, per_quarter, assemble, 0)


def pack_integrals(which, integrals, first_labels, second_labels, slab_irrep):
    first_width, second_width, slab = integrals.shape
    folds = LANES // second_width
    groups = first_width // folds
    per_step = 5
    pitch = -(-first_width // 8) * 8
    rows = (groups + groups // QUARTERS) * LANES
    smem = pl.BlockSpec(memory_space=pltpu.SMEM)
    whole = pl.BlockSpec(memory_space=pltpu.VMEM)
    return pl.pallas_call(
        functools.partial(pack_kernel, folds),
        grid=(second_width // per_step,),
        in_specs=[
            smem,
            smem,
            pl.BlockSpec((per_step, first_width, slab), lambda i: (i, 0, 0)),
            whole,
            whole,
            whole,
        ],
        out_specs=[whole, whole],
        out_shape=[
            jax.ShapeDtypeStruct((rows, LANES), jnp.bfloat16),
            jax.ShapeDtypeStruct((1, slab), jnp.int32),
        ],
        scratch_shapes=[
            pltpu.VMEM((slab, 2 * LANES), jnp.bfloat16),
            pltpu.VMEM((second_width * pitch, LANES), jnp.float32),
            pltpu.VMEM((second_width * pitch, LANES), jnp.float32),
            pltpu.VMEM((LANES, LANES), jnp.float32),
            pltpu.VMEM((LANES, LANES), jnp.float32),
        ],
        compiler_params=pltpu.CompilerParams(
            dimension_semantics=("arbitrary",), vmem_limit_bytes=VMEM_LIMIT
        ),
        cost_estimate=pl.CostEstimate(
            flops=2 * 2600 * slab * 256, bytes_accessed=6_000_000, transcendentals=0
        ),
        name="pack_integrals",
    )(
        which,
        second_labels,
        jnp.transpose(integrals, (1, 0, 2)),
        first_labels.reshape(first_width, 1),
        slab_irrep.reshape(1, slab),
        slab_irrep.reshape(slab, 1),
    )


def spread_kernel(folds, second_width, rest, parts, amp_ref, out_ref, wide, strided, stage):
    pairs, virt, _ = amp_ref.shape
    tiles = wide.shape[0]
    tall = virt // folds
    last = (tiles - 1) * LANES
    for p in range(pairs):
        for t in range(tiles):
            if t < tiles - 1:
                wide[t] = amp_ref[p, :, t * LANES : (t + 1) * LANES].astype(jnp.float32)
            else:
                wide[t] = jnp.zeros((virt, LANES), jnp.float32)
                wide[t, :, : virt - last] = amp_ref[p, :, last:].astype(jnp.float32)
        for t in range(tiles):
            for f in range(folds):
                strided[f, p * tall : (p + 1) * tall, t * LANES : (t + 1) * LANES] = wide[
                    t, pl.ds(f, tall, stride=folds), :
                ].astype(jnp.bfloat16)
    span = 2 * LANES
    source = iota((span, 1), 0)
    lane = iota((span, span), 1)
    for w in range(rest // 2):
        tile = (2 * second_width * w) // LANES
        offset = 2 * second_width * w - tile * LANES
        column = source - offset
        inside = (column >= 0) & (column < 2 * second_width)
        target = column + jnp.where(column >= second_width, LANES - second_width, 0)
        total = jnp.zeros((pairs * tall, span), jnp.float32)
        for f in range(folds):
            select = one_hot(lane == jnp.where(inside, target + f * second_width, -1))
            total = total + dot(strided[f, :, tile * LANES : tile * LANES + span], select)
        for a in range(2):
            outer, inner = divmod(2 * w + a, parts)
            stage[inner, pl.ds(outer, pairs * tall, stride=rest // parts), :] = total[
                :, a * LANES : (a + 1) * LANES
            ]
    owners, rows = out_ref.shape[1], out_ref.shape[3]
    for inner in range(parts):
        for p in range(pairs):
            for i in range(owners):
                at = (p * owners + i) * rows
                out_ref[inner, i, p] = stage[inner, at : at + rows, :].astype(jnp.bfloat16)


def spread_amplitudes(amplitudes, owners, outer, parts):
    pairs, virt, _ = amplitudes.shape
    rest = outer * parts
    second_width = virt // rest
    folds = LANES // second_width
    tiles = -(-virt // LANES)
    tall = virt // folds
    rows = tall // owners * outer
    whole = pl.BlockSpec(memory_space=pltpu.VMEM)
    return pl.pallas_call(
        functools.partial(spread_kernel, folds, second_width, rest, parts),
        in_specs=[whole],
        out_specs=whole,
        out_shape=jax.ShapeDtypeStruct((parts, owners, pairs, rows, LANES), jnp.bfloat16),
        scratch_shapes=[
            pltpu.VMEM((tiles, virt, LANES), jnp.float32),
            pltpu.VMEM((folds, pairs * tall, tiles * LANES), jnp.bfloat16),
            pltpu.VMEM((parts, pairs * tall * outer, LANES), jnp.float32),
        ],
        compiler_params=pltpu.CompilerParams(vmem_limit_bytes=VMEM_LIMIT),
        cost_estimate=pl.CostEstimate(
            flops=2 * 480 * 80 * 65536, bytes_accessed=8_000_000, transcendentals=0
        ),
        name="spread_amplitudes",
    )(amplitudes)


def contract_kernel(
    count, here_ref, amp_ref, labels_ref, own_ref, r1, r2, r3, l1, l2, l3, far_a, far_b,
    out_ref, turned, left, right, total_main, total_over,
):
    all_pairs, rows, _ = amp_ref.shape
    groups = rows // count
    tile = 16
    square = tile * tile
    order = iota((square, square), 0)
    swap = one_hot(iota((square, square), 1) == (order % tile) * tile + order // tile)

    def turn(k, carry):
        at = pl.multiple_of(k * tile, tile)
        for p in range(0, all_pairs, 2 * tile):
            blocks = [
                amp_ref[q : q + tile, pl.ds(at, tile), :].reshape(square, LANES)
                for q in (p, p + tile)
            ]
            done = dot(swap, jnp.concatenate(blocks, axis=1)).astype(jnp.bfloat16)
            for r in range(tile):
                group = k * (tile // count) + r // count
                for h in range(2):
                    turned[r % count, group, p + h * tile : p + (h + 1) * tile, :] = done[
                        r * tile : (r + 1) * tile, h * LANES : (h + 1) * LANES
                    ]
        return carry

    lax.fori_loop(0, rows // tile, turn, 0)

    width = groups * LANES
    per_quarter = width // QUARTERS
    quarter = iota((1, LANES), 1) // SPARE
    half = far_a.shape[0]
    for k, blocks in enumerate(
        ((own_ref,), (r1,), (l1,), (r2,), (l2,), (r3,), (l3,), (far_a, far_b))
    ):
        away = (0, 1, -1, 2, -2, 3, -3, 4)[k]
        which = lax.rem(here_ref[0] - away + 2 * count, count)
        if len(blocks) == 1:
            right[:, :LANES] = blocks[0][:width, :]
            spare = blocks[0][width:, :]
        else:
            right[:half, :LANES] = far_a[...]
            right[half:, :LANES] = far_b[: width - half, :]
            spare = far_b[width - half :, :]
        for q in range(QUARTERS):
            keep = one_hot(quarter == q)
            right[q * per_quarter : (q + 1) * per_quarter, LANES:] = spare * keep
        for c in range(groups):
            piece = turned[which, c]
            label = labels_ref[which, :, c * LANES : (c + 1) * LANES]
            for g in range(IRREPS):
                left[g * all_pairs : (g + 1) * all_pairs, c * LANES : (c + 1) * LANES] = (
                    piece * one_hot(label == g)
                )
        product = dot(left[...], right[...])
        if k == 0:
            total_main[...] = product[:, :LANES]
            total_over[...] = product[:, LANES:]
        else:
            total_main[...] += product[:, :LANES]
            total_over[...] += product[:, LANES:]

    spare = total_over[...]
    spare = spare + pltpu.roll(spare, 2 * SPARE, 1)
    total_over[...] = spare + pltpu.roll(spare, SPARE, 1)
    out_rows = out_ref.shape[0]
    pairs = 3
    owners = all_pairs // pairs
    pitch = out_rows // owners
    out_ref[...] = jnp.zeros_like(out_ref)
    for g in range(IRREPS):
        for p in range(pairs):
            out_ref[pl.ds(g * pairs + p, owners, stride=pitch), :] = total_main[
                pl.ds(g * all_pairs + p, owners, stride=pairs), :
            ]
    each = IRREPS // QUARTERS
    for g in range(each):
        for p in range(pairs):
            value = jnp.zeros((owners, LANES), jnp.float32)
            for q in range(QUARTERS):
                piece = total_over[pl.ds((q * each + g) * all_pairs + p, owners, stride=pairs), :]
                value = value + jnp.where(quarter == q, piece, 0.0)
            out_ref[pl.ds((IRREPS + g) * pairs + p, owners, stride=pitch), :] = value


def contract(here, amplitudes, labels, blocks, count, pairs):
    all_pairs, rows, _ = amplitudes.shape
    groups = rows // count
    owners = all_pairs // pairs
    pitch = -(-(IRREPS + IRREPS // QUARTERS) * pairs // 8) * 8
    whole = pl.BlockSpec(memory_space=pltpu.VMEM)
    return pl.pallas_call(
        functools.partial(contract_kernel, count),
        in_specs=[pl.BlockSpec(memory_space=pltpu.SMEM)] + [whole] * 11,
        out_specs=whole,
        out_shape=jax.ShapeDtypeStruct((owners * pitch, LANES), jnp.float32),
        scratch_shapes=[
            pltpu.VMEM((count, groups, all_pairs, LANES), jnp.bfloat16),
            pltpu.VMEM((IRREPS * all_pairs, groups * LANES), jnp.bfloat16),
            pltpu.VMEM((groups * LANES, 2 * LANES), jnp.bfloat16),
            pltpu.VMEM((IRREPS * all_pairs, LANES), jnp.float32),
            pltpu.VMEM((IRREPS * all_pairs, LANES), jnp.float32),
        ],
        compiler_params=pltpu.CompilerParams(vmem_limit_bytes=VMEM_LIMIT),
        cost_estimate=pl.CostEstimate(
            flops=2 * 768 * 20480 * 256, bytes_accessed=11_000_000, transcendentals=0
        ),
        name="contract",
    )(here, amplitudes, labels, *blocks)


def unpack_kernel(pairs, round_ref, parts_ref, rank_ref, slab_ref, out_ref):
    rows = parts_ref.shape[1]
    slab = slab_ref.shape[1]
    summed = parts_ref[0]
    for k in range(1, parts_ref.shape[0]):
        summed = summed + parts_ref[k]
    irrep = slab_ref[...]
    rank = rank_ref[...] - round_ref[0] * CAP
    each = IRREPS // QUARTERS
    inside = (rank >= 0) & (rank < CAP)
    spare = rank >= LANES
    target = jnp.where(spare, (irrep // each) * SPARE + rank - LANES, rank)
    target = jnp.where(inside, target, -1)
    pick = jnp.where(iota((LANES, slab), 0) == target, 1.0, 0.0)
    values = jnp.dot(
        summed, pick, preferred_element_type=jnp.float32, precision=lax.Precision.HIGHEST
    )
    first = jnp.where(spare, (IRREPS + irrep % each) * pairs, irrep * pairs)
    row = iota((rows, slab), 0)
    for p in range(pairs):
        out_ref[p : p + 1, :] = jnp.sum(
            jnp.where(row == first + p, values, 0.0), axis=0, keepdims=True
        )


def unpack(which, parts, rank, slab_irrep, pairs):
    slab = slab_irrep.shape[0]
    whole = pl.BlockSpec(memory_space=pltpu.VMEM)
    return pl.pallas_call(
        functools.partial(unpack_kernel, pairs),
        in_specs=[pl.BlockSpec(memory_space=pltpu.SMEM), whole, whole, whole],
        out_specs=whole,
        out_shape=jax.ShapeDtypeStruct((pairs, slab), jnp.float32),
        compiler_params=pltpu.CompilerParams(vmem_limit_bytes=VMEM_LIMIT),
        name="unpack",
    )(which, parts, rank, slab_irrep.reshape(1, slab))


def local(amplitudes, integrals, virt_irrep, slab_irrep):
    pairs = amplitudes.shape[0]
    owners = lax.axis_size("va")
    count = lax.axis_size("vb")
    parts = lax.axis_size("occ")
    first_width, second_width, _ = integrals.shape
    folds = LANES // second_width
    groups = first_width // folds
    here = lax.axis_index("vb")
    part = lax.axis_index("occ")

    first_labels = lax.dynamic_slice_in_dim(
        virt_irrep, lax.axis_index("va") * first_width, first_width, 0
    )
    second_labels = lax.dynamic_index_in_dim(
        virt_irrep.reshape(count, parts, second_width), part, 1, keepdims=False
    )
    own_labels = lax.dynamic_index_in_dim(second_labels, here, 0, keepdims=False)
    labels = jnp.bitwise_xor(
        first_labels.reshape(1, groups, folds, 1), second_labels.reshape(count, 1, 1, second_width)
    ).reshape(count, groups, folds * second_width)
    labels = jnp.pad(
        labels, ((0, 0), (0, 0), (0, LANES - folds * second_width)), constant_values=-1
    ).reshape(count, 1, groups * LANES)

    up = [(i, (i + 1) % count) for i in range(count)]
    down = [(i, (i - 1) % count) for i in range(count)]

    def blocks_of(which):
        packed, rank = pack_integrals(which, integrals, first_labels, own_labels, slab_irrep)
        r1 = lax.ppermute(packed, "vb", up)
        l1 = lax.ppermute(packed, "vb", down)
        r2 = lax.ppermute(r1, "vb", up)
        l2 = lax.ppermute(l1, "vb", down)
        r3 = lax.ppermute(r2, "vb", up)
        l3 = lax.ppermute(l2, "vb", down)
        half = packed.shape[0] // 2
        far_a = lax.ppermute(r3[:half], "vb", up)
        far_b = lax.ppermute(l3[half:], "vb", down)
        return (packed, r1, r2, r3, l1, l2, l3, far_a, far_b), rank

    def finish(which, blocks, rank, arrived):
        partial = contract(here.reshape(1), arrived, labels, blocks, count, pairs)
        partial = partial.reshape(parts * owners, -1, LANES)
        summands = lax.all_to_all(partial, SOURCES, split_axis=0, concat_axis=0, tiled=True)
        return unpack(which, summands, rank, slab_irrep, pairs)

    first = jnp.zeros((1,), jnp.int32)
    blocks, rank = blocks_of(first)
    spread = spread_amplitudes(amplitudes, owners, count, parts)
    sent = spread.reshape((parts * owners,) + spread.shape[2:])
    arrived = lax.all_to_all(sent, SOURCES, split_axis=0, concat_axis=0, tiled=True)
    arrived = arrived.reshape((parts * owners * pairs,) + spread.shape[3:])
    result = finish(first, blocks, rank, arrived)
    largest = jnp.max(rank)

    def more(carry):
        return carry[0] * CAP <= largest

    def step(carry):
        which = carry[0].reshape(1)
        blocks, rank = blocks_of(which)
        return carry[0] + 1, carry[1] + finish(which, blocks, rank, arrived)

    return lax.while_loop(more, step, (jnp.int32(1), result))[1]


def solution(mesh):
    return jax.shard_map(
        local,
        mesh=mesh,
        in_specs=(P(("va", "vb", "occ"), None, None), P("va", ("vb", "occ"), None), P(), P()),
        out_specs=P(("va", "vb", "occ"), None),
        check_vma=False,
    )
```

```python
import functools

import jax
import jax.numpy as jnp
from jax import lax
from jax.experimental import pallas as pl
from jax.experimental.pallas import tpu as pltpu
from jax.sharding import PartitionSpec as P

LANES = 128
IRREPS = 8
SPARE = 32
CAP = LANES + SPARE
QUARTERS = LANES // SPARE
VMEM_LIMIT = 56 * 1024 * 1024
SOURCES = ("occ", "va")
AWAYS = (0, 1, 7, 2, 6, 5, 3, 4)


def iota(shape, axis):
    return lax.broadcasted_iota(jnp.int32, shape, axis)


def one_hot(hits):
    return jnp.where(hits, 1.0, 0.0).astype(jnp.bfloat16)


def dot(a, b):
    return jnp.dot(a, b, preferred_element_type=jnp.float32)


def pack_kernel(
    folds, round_ref, second_ref, block_ref, first_ref, row_ref, after_ref,
    low_ref, high_ref, rank_ref, onehot, firsts, masked, main, over, stage_main, stage_over,
):
    del after_ref
    step = pl.program_id(0)
    per_step, first_width, slab = block_ref.shape
    second_width = per_step * pl.num_programs(0)
    pitch = masked.shape[0] // per_step
    groups = first_width // folds
    square = (LANES, LANES)

    def turned(vector):
        return jnp.transpose(jnp.broadcast_to(vector, square))

    @pl.when(step == 0)
    def _():
        masked[...] = jnp.zeros_like(masked)
        firsts[...] = turned(first_ref[...])[: firsts.shape[0]]
        offset = (round_ref[0] * CAP).astype(jnp.float32)
        before = one_hot(iota(square, 0) < iota(square, 1))
        lane = iota((LANES, 2 * LANES), 1).astype(jnp.float32)
        base = jnp.zeros((IRREPS, 1), jnp.float32)
        for k in range(slab // LANES):
            at = slice(k * LANES, (k + 1) * LANES)
            own = iota((IRREPS, LANES), 0).astype(jnp.float32) == row_ref[:, at]
            member = jnp.where(own, 1.0, 0.0)
            count = dot(member.astype(jnp.bfloat16), before) + base
            rank = jnp.sum(jnp.where(own, count, 0.0), axis=0, keepdims=True)
            rank_ref[:, at] = rank.astype(jnp.int32)
            base = base + jnp.sum(member, axis=1, keepdims=True)
            column = turned(rank) - offset
            onehot[at, :] = one_hot(lane == jnp.concatenate([column, column], axis=1))

    for k in range(per_step):
        second = second_ref[step * per_step + k]
        wanted = jnp.bitwise_xor(firsts[...].astype(jnp.int32), second).astype(jnp.float32)
        wanted = wanted[:first_width]
        for t in range(slab // LANES):
            at = slice(t * LANES, (t + 1) * LANES)
            allowed = wanted == row_ref[:, at]
            values = jnp.where(allowed, block_ref[k, :, at].astype(jnp.float32), 0.0)
            masked[k * pitch : k * pitch + first_width, at] = values.astype(jnp.bfloat16)
    packed = dot(masked[...], onehot[...])
    start = pl.multiple_of(step * per_step * pitch, 8)
    main[pl.ds(start, per_step * pitch), :] = packed[:, :LANES]
    over[pl.ds(start, per_step * pitch), :] = packed[:, LANES:]

    @pl.when(step == pl.num_programs(0) - 1)
    def _():
        stage_main[...] = jnp.zeros_like(stage_main)
        stage_over[...] = jnp.zeros_like(stage_over)
        per_quarter = groups // QUARTERS
        low = iota(square, 1) < SPARE

        split = groups // 2
        for e in range(per_quarter):
            spare = jnp.zeros(square, jnp.float32)
            for q in range(QUARTERS):
                group = q * per_quarter + e
                for f in range(folds):
                    rows = pl.ds(group * folds + f, second_width, stride=pitch)
                    stage_main[q, pl.ds(f * second_width, second_width), :] = main[rows, :]
                    stage_over[q, pl.ds(f * second_width, second_width), :] = over[rows, :]
                packed = stage_main[q].astype(jnp.bfloat16)
                if group < split:
                    low_ref[group] = packed
                else:
                    high_ref[group - split] = packed
                piece = jnp.where(low, stage_over[q], 0.0)
                spare = spare + (piece if q == 0 else pltpu.roll(piece, q * SPARE, 1))
            spare = spare.astype(jnp.bfloat16)
            if e < per_quarter // 2:
                low_ref[split + e] = spare
            else:
                high_ref[split + e - per_quarter // 2] = spare


def pack_integrals(which, integrals, first_labels, second_labels, slab_irrep, after):
    first_width, second_width, slab = integrals.shape
    folds = LANES // second_width
    groups = first_width // folds
    per_step = 5
    pitch = -(-first_width // 16) * 16
    low = groups // 2 + groups // QUARTERS // 2
    high = groups + groups // QUARTERS - low
    smem = pl.BlockSpec(memory_space=pltpu.SMEM)
    whole = pl.BlockSpec(memory_space=pltpu.VMEM)
    firsts = jnp.pad(first_labels, (0, LANES - first_width)).astype(jnp.float32)
    return pl.pallas_call(
        functools.partial(pack_kernel, folds),
        grid=(second_width // per_step,),
        in_specs=[
            smem,
            smem,
            pl.BlockSpec((per_step, first_width, slab), lambda i: (i, 0, 0)),
            whole,
            whole,
            pl.BlockSpec(memory_space=pl.ANY),
        ],
        out_specs=[whole, whole, whole],
        out_shape=[
            jax.ShapeDtypeStruct((low, LANES, LANES), jnp.bfloat16),
            jax.ShapeDtypeStruct((high, LANES, LANES), jnp.bfloat16),
            jax.ShapeDtypeStruct((1, slab), jnp.int32),
        ],
        scratch_shapes=[
            pltpu.VMEM((slab, 2 * LANES), jnp.bfloat16),
            pltpu.VMEM((pitch, LANES), jnp.float32),
            pltpu.VMEM((per_step * pitch, slab), jnp.bfloat16),
            pltpu.VMEM((second_width * pitch, LANES), jnp.float32),
            pltpu.VMEM((second_width * pitch, LANES), jnp.float32),
            pltpu.VMEM((QUARTERS, LANES, LANES), jnp.float32),
            pltpu.VMEM((QUARTERS, LANES, LANES), jnp.float32),
        ],
        compiler_params=pltpu.CompilerParams(
            dimension_semantics=("arbitrary",), vmem_limit_bytes=VMEM_LIMIT
        ),
        cost_estimate=pl.CostEstimate(
            flops=2 * 2600 * slab * 256, bytes_accessed=6_000_000, transcendentals=0
        ),
        name="pack_integrals",
    )(
        which,
        second_labels,
        jnp.transpose(integrals, (1, 0, 2)),
        firsts.reshape(1, LANES),
        slab_irrep.astype(jnp.float32).reshape(1, slab),
        after,
    )


def spread_kernel(
    folds, second_width, rest, parts, here_ref, amp_ref, out_ref,
    wide, strided, shifted, stage,
):
    virt = amp_ref.shape[1]
    tiles = wide.shape[0]
    tall = virt // folds
    last = (tiles - 1) * LANES
    early = iota((tall, LANES), 1) < LANES // 2
    for t in range(tiles):
        if t < tiles - 1:
            wide[t] = amp_ref[0, :, t * LANES : (t + 1) * LANES].astype(jnp.float32)
        else:
            wide[t] = jnp.zeros((virt, LANES), jnp.float32)
            wide[t, :, : virt - last] = amp_ref[0, :, last:].astype(jnp.float32)
    for f in range(folds):
        held = None
        for t in range(tiles):
            piece = wide[t, pl.ds(f, tall, stride=folds), :]
            strided[f, :, t * LANES : (t + 1) * LANES] = piece.astype(jnp.bfloat16)
            rolled = pltpu.roll(piece, LANES // 2, 1)
            if t > 0:
                shifted[f, :, (t - 1) * LANES : t * LANES] = jnp.where(
                    early, held, rolled
                ).astype(jnp.bfloat16)
            held = rolled
    span = 2 * second_width
    source = iota((LANES, 1), 0)
    lane = iota((LANES, 2 * LANES), 1)
    slots = rest // parts // 2
    for w in range(rest // 2):
        tile, offset = divmod(span * w, LANES)
        held = strided
        if offset + span > LANES:
            held, offset = shifted, offset - LANES // 2
        column = source - offset
        inside = (column >= 0) & (column < span)
        target = column + jnp.where(column >= second_width, LANES - second_width, 0)
        target = jnp.where(inside, target, -LANES)
        at = slice(tile * LANES, (tile + 1) * LANES)
        select = jnp.concatenate(
            [one_hot(lane == target + f * second_width) for f in range(folds)], axis=0
        )
        total = dot(jnp.concatenate([held[f, :, at] for f in range(folds)], axis=1), select)
        for a in range(2):
            outer, inner = divmod(2 * w + a, parts)
            away = lax.rem(outer - here_ref[0] + rest // parts, rest // parts)
            place = sum(jnp.where(away == k, AWAYS.index(k), 0) for k in AWAYS)
            half = place // slots
            stage[half, inner, pl.ds(place - half * slots, tall, stride=slots), :] = total[
                :, a * LANES : (a + 1) * LANES
            ]
    owners = out_ref.shape[1]
    rows = out_ref.shape[3] // 2
    for inner in range(parts):
        for i in range(owners):
            for half in range(2):
                out_ref[inner, i, 0, half * rows : (half + 1) * rows] = stage[
                    half, inner, i * rows : (i + 1) * rows, :
                ].astype(jnp.bfloat16)


def spread_amplitudes(here, amplitudes, owners, outer, parts):
    pairs, virt, _ = amplitudes.shape
    rest = outer * parts
    second_width = virt // rest
    folds = LANES // second_width
    tiles = -(-virt // LANES)
    tall = virt // folds
    rows = tall // owners * outer
    return pl.pallas_call(
        functools.partial(spread_kernel, folds, second_width, rest, parts),
        grid=(pairs,),
        in_specs=[
            pl.BlockSpec(memory_space=pltpu.SMEM),
            pl.BlockSpec((1, virt, virt), lambda p: (p, 0, 0)),
        ],
        out_specs=pl.BlockSpec((parts, owners, 1, rows, LANES), lambda p: (0, 0, p, 0, 0)),
        out_shape=jax.ShapeDtypeStruct((parts, owners, pairs, rows, LANES), jnp.bfloat16),
        scratch_shapes=[
            pltpu.VMEM((tiles, virt, LANES), jnp.float32),
            pltpu.VMEM((folds, tall, tiles * LANES), jnp.bfloat16),
            pltpu.VMEM((folds, tall, (tiles - 1) * LANES), jnp.bfloat16),
            pltpu.VMEM((2, parts, tall * outer // 2, LANES), jnp.float32),
        ],
        compiler_params=pltpu.CompilerParams(
            dimension_semantics=("arbitrary",), vmem_limit_bytes=VMEM_LIMIT
        ),
        cost_estimate=pl.CostEstimate(
            flops=2 * 480 * 80 * 65536, bytes_accessed=8_000_000, transcendentals=0
        ),
        name="spread_amplitudes",
    )(here, amplitudes)


def masked_rows(left, at, piece, label):
    tall = piece.shape[0]
    for g in range(IRREPS):
        left[g * tall : (g + 1) * tall, at : at + LANES] = piece * one_hot(label == g)


def contract_kernel(tile, slots, shards, half, amp_ref, labels_ref, *refs):
    refs = list(refs)
    first = half == 0
    start_ref = None if first else refs.pop(0)
    blocks = [(refs[2 * k], refs[2 * k + 1]) for k in range(shards)]
    refs = refs[2 * shards :]
    out_ref = refs.pop(0)
    rest_ref = refs.pop(0) if shards < slots else None
    (amps, turned, left_a, left_b, right, spares, swap, total,
     amp_sems, block_sems, spare_sems, start_sem) = refs
    all_pairs = amps.shape[1]
    steps = amps.shape[0]
    groups = right.shape[0]
    per_quarter = groups // QUARTERS
    each = tile // slots
    square = tile * tile

    def amp_copy(k):
        at = pl.ds(half * steps * tile + k * tile, tile)
        return pltpu.make_async_copy(amp_ref.at[:, at], amps.at[k], amp_sems.at[k])

    copies = []
    split, cut = groups // 2, per_quarter // 2
    for k, pair in enumerate(blocks):
        for h, block in enumerate(pair):
            copies.append(
                pltpu.make_async_copy(
                    block.at[pl.ds(0, split)],
                    right.at[pl.ds(h * split, split), k, :, pl.ds(0, LANES)],
                    block_sems.at[2 * k + h],
                )
            )
            count = (cut, per_quarter - cut)[h]
            copies.append(
                pltpu.make_async_copy(
                    block.at[pl.ds(split, count)],
                    spares.at[k, pl.ds(h * cut, count)],
                    spare_sems.at[2 * k + h],
                )
            )
    if not first:
        copies.append(pltpu.make_async_copy(start_ref, total, start_sem))
    amp_copies = [amp_copy(k) for k in range(steps)]
    amp_copies[0].start()
    for copy in copies:
        copy.start()
    for copy in amp_copies[1:]:
        copy.start()
    order = iota((square, square), 0)
    swap[...] = one_hot(iota((square, square), 1) == (order % tile) * tile + order // tile)
    if first:
        total[...] = jnp.zeros_like(total)
    quarter = iota((1, LANES), 1) // SPARE

    def build(k, left):
        amp_copies[k].wait()
        for p in range(0, all_pairs, 2 * tile):
            pieces = [amps[k, q : q + tile].reshape(square, LANES) for q in (p, p + tile)]
            done = dot(swap[...], jnp.concatenate(pieces, axis=1)).astype(jnp.bfloat16)
            for r in range(tile):
                for h in range(2):
                    turned[k % 2, r, p + h * tile : p + (h + 1) * tile, :] = done[
                        r * tile : (r + 1) * tile, h * LANES : (h + 1) * LANES
                    ]
        for r in range(tile):
            group, slot = divmod(r, slots)
            if slot < shards:
                label = labels_ref[k * tile + r : k * tile + r + 1, :]
                masked_rows(left, (group * shards + slot) * LANES, turned[k % 2, r], label)
            else:
                rest_ref[k * each + group] = turned[k % 2, r]

    lefts = (left_a, left_b)
    build(0, left_a)
    for copy in copies:
        copy.wait()
    for c in range(groups):
        keep = one_hot(quarter == c // per_quarter)
        for k in range(shards):
            right[c, k, :, LANES:] = spares[k, c % per_quarter] * keep
    for k in range(steps):
        if k + 1 < steps:
            build(k + 1, lefts[(k + 1) % 2])
        block = right[k * each : (k + 1) * each].reshape(each * shards * LANES, 2 * LANES)
        total[...] += dot(lefts[k % 2][...], block)
    out_ref[...] = total[...]


def contract(amplitudes, labels, start, blocks, half):
    all_pairs, rows, _ = amplitudes.shape
    tile = 16
    slots = 4
    shards = len(blocks)
    groups = rows // (2 * slots)
    per_quarter = groups // QUARTERS
    whole = pl.BlockSpec(memory_space=pltpu.VMEM)
    hbm = pl.BlockSpec(memory_space=pl.ANY)
    steps = rows // 2 // tile
    tall = IRREPS * all_pairs
    wide = tile // slots * shards * LANES
    operands = (() if half == 0 else (start,)) + tuple(sum(blocks, ()))
    out_shape = [jax.ShapeDtypeStruct((tall, 2 * LANES), jnp.float32)]
    if shards < slots:
        out_shape.append(jax.ShapeDtypeStruct((groups, all_pairs, LANES), jnp.bfloat16))
    return pl.pallas_call(
        functools.partial(contract_kernel, tile, slots, shards, half),
        in_specs=[hbm, whole] + [hbm] * len(operands),
        out_specs=[whole] * len(out_shape),
        out_shape=out_shape,
        scratch_shapes=[
            pltpu.VMEM((steps, all_pairs, tile, LANES), jnp.bfloat16),
            pltpu.VMEM((2, tile, all_pairs, LANES), jnp.bfloat16),
            pltpu.VMEM((tall, wide), jnp.bfloat16),
            pltpu.VMEM((tall, wide), jnp.bfloat16),
            pltpu.VMEM((groups, shards, LANES, 2 * LANES), jnp.bfloat16),
            pltpu.VMEM((shards, per_quarter, LANES, LANES), jnp.bfloat16),
            pltpu.VMEM((tile * tile, tile * tile), jnp.bfloat16),
            pltpu.VMEM((tall, 2 * LANES), jnp.float32),
            pltpu.SemaphoreType.DMA((steps,)),
            pltpu.SemaphoreType.DMA((2 * shards,)),
            pltpu.SemaphoreType.DMA((2 * shards,)),
            pltpu.SemaphoreType.DMA,
        ],
        compiler_params=pltpu.CompilerParams(vmem_limit_bytes=VMEM_LIMIT),
        cost_estimate=pl.CostEstimate(
            flops=2 * 768 * 10240 * 256, bytes_accessed=6_000_000, transcendentals=0
        ),
        name="contract",
    )(amplitudes, labels, *operands)


def last_kernel(pairs, slots, rest_ref, labels_ref, start_ref, low_ref, high_ref, out_ref,
                left, right, main, over):
    groups, all_pairs, _ = rest_ref.shape
    per_quarter = groups // QUARTERS
    split, cut = groups // 2, per_quarter // 2
    quarter = iota((1, LANES), 1) // SPARE
    for c in range(groups):
        row = c * slots + slots - 1
        masked_rows(left, c * LANES, rest_ref[c], labels_ref[row : row + 1, :])
        at = slice(c * LANES, (c + 1) * LANES)
        right[at, :LANES] = low_ref[c] if c < split else high_ref[c - split]
        e = c % per_quarter
        spare = low_ref[split + e] if e < cut else high_ref[split + e - cut]
        right[at, LANES:] = spare * one_hot(quarter == c // per_quarter)
    total = start_ref[...] + dot(left[...], right[...])
    main[...] = total[:, :LANES]
    spare = total[:, LANES:]
    spare = spare + pltpu.roll(spare, 2 * SPARE, 1)
    over[...] = spare + pltpu.roll(spare, SPARE, 1)
    owners = all_pairs // pairs
    pitch = out_ref.shape[0] // owners
    out_ref[...] = jnp.zeros_like(out_ref)
    for g in range(IRREPS):
        for p in range(pairs):
            out_ref[pl.ds(g * pairs + p, owners, stride=pitch), :] = main[
                pl.ds(g * all_pairs + p, owners, stride=pairs), :
            ]
    per = IRREPS // QUARTERS
    for g in range(per):
        for p in range(pairs):
            value = jnp.zeros((owners, LANES), jnp.float32)
            for q in range(QUARTERS):
                piece = over[pl.ds((q * per + g) * all_pairs + p, owners, stride=pairs), :]
                value = value + jnp.where(quarter == q, piece, 0.0)
            out_ref[pl.ds((IRREPS + g) * pairs + p, owners, stride=pitch), :] = value


def contract_last(rest, labels, start, low, high, pairs):
    groups, all_pairs, _ = rest.shape
    owners = all_pairs // pairs
    pitch = -(-(IRREPS + IRREPS // QUARTERS) * pairs // 8) * 8
    whole = pl.BlockSpec(memory_space=pltpu.VMEM)
    tall = IRREPS * all_pairs
    return pl.pallas_call(
        functools.partial(last_kernel, pairs, labels.shape[0] // groups),
        in_specs=[whole] * 5,
        out_specs=whole,
        out_shape=jax.ShapeDtypeStruct((owners * pitch, LANES), jnp.float32),
        scratch_shapes=[
            pltpu.VMEM((tall, groups * LANES), jnp.bfloat16),
            pltpu.VMEM((groups * LANES, 2 * LANES), jnp.bfloat16),
            pltpu.VMEM((tall, LANES), jnp.float32),
            pltpu.VMEM((tall, LANES), jnp.float32),
        ],
        compiler_params=pltpu.CompilerParams(vmem_limit_bytes=VMEM_LIMIT),
        cost_estimate=pl.CostEstimate(
            flops=2 * 768 * 2560 * 256, bytes_accessed=3_000_000, transcendentals=0
        ),
        name="contract_last",
    )(rest, labels, start, low, high)


def unpack_kernel(pairs, round_ref, parts_ref, rank_ref, slab_ref, out_ref):
    rows = parts_ref.shape[1]
    slab = slab_ref.shape[1]
    summed = parts_ref[0]
    for k in range(1, parts_ref.shape[0]):
        summed = summed + parts_ref[k]
    irrep = slab_ref[...]
    rank = rank_ref[...] - round_ref[0] * CAP
    each = IRREPS // QUARTERS
    inside = (rank >= 0) & (rank < CAP)
    spare = rank >= LANES
    target = jnp.where(spare, (irrep // each) * SPARE + rank - LANES, rank)
    target = jnp.where(inside, target, -1)
    pick = jnp.where(iota((LANES, slab), 0) == target, 1.0, 0.0)
    values = jnp.dot(
        summed, pick, preferred_element_type=jnp.float32, precision=lax.Precision.HIGHEST
    )
    first = jnp.where(spare, (IRREPS + irrep % each) * pairs, irrep * pairs)
    row = iota((rows, slab), 0)
    for p in range(pairs):
        out_ref[p : p + 1, :] = jnp.sum(
            jnp.where(row == first + p, values, 0.0), axis=0, keepdims=True
        )


def unpack(which, parts, rank, slab_irrep, pairs):
    slab = slab_irrep.shape[0]
    whole = pl.BlockSpec(memory_space=pltpu.VMEM)
    return pl.pallas_call(
        functools.partial(unpack_kernel, pairs),
        in_specs=[pl.BlockSpec(memory_space=pltpu.SMEM), whole, whole, whole],
        out_specs=whole,
        out_shape=jax.ShapeDtypeStruct((pairs, slab), jnp.float32),
        compiler_params=pltpu.CompilerParams(vmem_limit_bytes=VMEM_LIMIT),
        name="unpack",
    )(which, parts, rank, slab_irrep.reshape(1, slab))


def local(amplitudes, integrals, virt_irrep, slab_irrep):
    pairs = amplitudes.shape[0]
    owners = lax.axis_size("va")
    count = lax.axis_size("vb")
    parts = lax.axis_size("occ")
    first_width, second_width, _ = integrals.shape
    folds = LANES // second_width
    groups = first_width // folds
    here = lax.axis_index("vb")
    part = lax.axis_index("occ")

    first_labels = lax.dynamic_slice_in_dim(
        virt_irrep, lax.axis_index("va") * first_width, first_width, 0
    )
    second_labels = lax.dynamic_index_in_dim(
        virt_irrep.reshape(count, parts, second_width), part, 1, keepdims=False
    )
    own_labels = lax.dynamic_index_in_dim(second_labels, here, 0, keepdims=False)
    order = lax.rem(here + jnp.array(AWAYS, jnp.int32), count)
    labels = jnp.bitwise_xor(
        first_labels.reshape(groups, 1, folds, 1),
        jnp.take(second_labels, order, axis=0).reshape(1, count, 1, second_width),
    ).reshape(groups, count, folds * second_width)
    labels = jnp.pad(
        labels, ((0, 0), (0, 0), (0, LANES - folds * second_width)), constant_values=-1
    )
    near_labels = labels[:, : count // 2].reshape(-1, LANES)
    far_labels = labels[:, count // 2 :].reshape(-1, LANES)

    up = [(i, (i + 1) % count) for i in range(count)]
    down = [(i, (i - 1) % count) for i in range(count)]

    def shifted(pair, perm):
        return tuple(lax.ppermute(block, "vb", perm) for block in pair)

    def blocks_of(which, after):
        *packed, rank = pack_integrals(
            which, integrals, first_labels, own_labels, slab_irrep, after
        )
        r1, l1 = shifted(packed, up), shifted(packed, down)
        r2, l2 = shifted(r1, up), shifted(l1, down)
        r3, l3 = shifted(r2, up), shifted(l2, down)
        return (tuple(packed), l1, r1, l2), (r2, r3, l3), rank

    def finish(which, near, middle, rank, arrived):
        (start,) = contract(arrived, near_labels, None, near, 0)
        up_end, down_end, start = lax.optimization_barrier((middle[1][0], middle[2][1], start))
        far = lax.ppermute(up_end, "vb", up), lax.ppermute(down_end, "vb", down)
        start, rest = contract(arrived, far_labels, start, middle, 1)
        partial = contract_last(rest, far_labels, start, *far, pairs)
        partial = partial.reshape(parts * owners, -1, LANES)
        summands = lax.all_to_all(partial, SOURCES, split_axis=0, concat_axis=0, tiled=True)
        return unpack(which, summands, rank, slab_irrep, pairs)

    first = jnp.zeros((1,), jnp.int32)
    spread = spread_amplitudes(here.reshape(1), amplitudes, owners, count, parts)
    sent = spread.reshape((parts * owners,) + spread.shape[2:])
    arrived = lax.all_to_all(sent, SOURCES, split_axis=0, concat_axis=0, tiled=True)
    arrived = arrived.reshape((parts * owners * pairs,) + spread.shape[3:])
    near, middle, rank = blocks_of(first, spread)
    result = finish(first, near, middle, rank, arrived)
    largest = jnp.max(rank)

    def more(carry):
        return carry[0] * CAP <= largest

    def step(carry):
        which = carry[0].reshape(1)
        near, middle, rank = blocks_of(which, spread)
        return carry[0] + 1, carry[1] + finish(which, near, middle, rank, arrived)

    return lax.while_loop(more, step, (jnp.int32(1), result))[1]


def solution(mesh):
    return jax.shard_map(
        local,
        mesh=mesh,
        in_specs=(P(("va", "vb", "occ"), None, None), P("va", ("vb", "occ"), None), P(), P()),
        out_specs=P(("va", "vb", "occ"), None),
        check_vma=False,
    )
```

```python
import functools

import jax
import jax.numpy as jnp
from jax import lax
from jax.experimental import pallas as pl
from jax.experimental.pallas import tpu as pltpu
from jax.sharding import PartitionSpec as P

LANES = 128
IRREPS = 8
SPARE = 32
CAP = LANES + SPARE
QUARTERS = LANES // SPARE
VMEM_LIMIT = 56 * 1024 * 1024
SOURCES = ("occ", "va")
AWAYS = (0, 1, 7, 2, 6, 5, 3, 4)


def iota(shape, axis):
    return lax.broadcasted_iota(jnp.int32, shape, axis)


def one_hot(hits):
    return jnp.where(hits, 1.0, 0.0).astype(jnp.bfloat16)


def dot(a, b):
    return jnp.dot(a, b, preferred_element_type=jnp.float32)


def pack_kernel(
    folds, round_ref, second_ref, block_ref, first_ref, row_ref, after_ref,
    low_ref, high_ref, rank_ref, onehot, firsts, masked, part_main, part_over, main, over,
):
    del after_ref
    step = pl.program_id(0)
    per_step, first_width, slab = block_ref.shape
    second_width = per_step * pl.num_programs(0)
    pitch = masked.shape[0] // per_step
    groups = first_width // folds
    square = (LANES, LANES)

    def turned(vector):
        return jnp.transpose(jnp.broadcast_to(vector, square))

    @pl.when(step == 0)
    def _():
        masked[...] = jnp.zeros_like(masked)
        for pad in range(folds * second_width, LANES):
            rows = pl.ds(pad, groups, stride=LANES)
            main[rows, :] = jnp.zeros((groups, LANES), jnp.float32)
            over[rows, :] = jnp.zeros((groups, LANES), jnp.float32)
        firsts[...] = turned(first_ref[...])[: firsts.shape[0]]
        offset = (round_ref[0] * CAP).astype(jnp.float32)
        before = one_hot(iota(square, 0) < iota(square, 1))
        lane = iota((LANES, 2 * LANES), 1).astype(jnp.float32)
        base = jnp.zeros((IRREPS, 1), jnp.float32)
        for k in range(slab // LANES):
            at = slice(k * LANES, (k + 1) * LANES)
            own = iota((IRREPS, LANES), 0).astype(jnp.float32) == row_ref[:, at]
            member = jnp.where(own, 1.0, 0.0)
            count = dot(member.astype(jnp.bfloat16), before) + base
            rank = jnp.sum(jnp.where(own, count, 0.0), axis=0, keepdims=True)
            rank_ref[:, at] = rank.astype(jnp.int32)
            base = base + jnp.sum(member, axis=1, keepdims=True)
            column = turned(rank) - offset
            onehot[at, :] = one_hot(lane == jnp.concatenate([column, column], axis=1))

    for k in range(per_step):
        second = second_ref[step * per_step + k]
        wanted = jnp.bitwise_xor(firsts[...].astype(jnp.int32), second).astype(jnp.float32)
        wanted = wanted[:first_width]
        for t in range(slab // LANES):
            at = slice(t * LANES, (t + 1) * LANES)
            allowed = wanted == row_ref[:, at]
            values = jnp.where(allowed, block_ref[k, :, at].astype(jnp.float32), 0.0)
            masked[k * pitch : k * pitch + first_width, at] = values.astype(jnp.bfloat16)
    packed = dot(masked[...], onehot[...])
    part_main[...] = packed[:, :LANES]
    part_over[...] = packed[:, LANES:]
    for k in range(per_step):
        d = step * per_step + k
        for f in range(folds):
            source = pl.ds(k * pitch + f, groups, stride=folds)
            target = pl.ds(f * second_width + d, groups, stride=LANES)
            main[target, :] = part_main[source, :]
            over[target, :] = part_over[source, :]

    @pl.when(step == pl.num_programs(0) - 1)
    def _():
        per_quarter = groups // QUARTERS
        low = iota(square, 1) < SPARE
        split = groups // 2
        for e in range(per_quarter):
            spare = jnp.zeros(square, jnp.float32)
            for q in range(QUARTERS):
                group = q * per_quarter + e
                rows = slice(group * LANES, (group + 1) * LANES)
                packed = main[rows, :].astype(jnp.bfloat16)
                if group < split:
                    low_ref[group] = packed
                else:
                    high_ref[group - split] = packed
                piece = jnp.where(low, over[rows, :], 0.0)
                spare = spare + (piece if q == 0 else pltpu.roll(piece, q * SPARE, 1))
            spare = spare.astype(jnp.bfloat16)
            if e < per_quarter // 2:
                low_ref[split + e] = spare
            else:
                high_ref[split + e - per_quarter // 2] = spare


def pack_integrals(which, integrals, first_labels, second_labels, slab_irrep, after):
    first_width, second_width, slab = integrals.shape
    folds = LANES // second_width
    groups = first_width // folds
    per_step = 5
    pitch = -(-first_width // 16) * 16
    low = groups // 2 + groups // QUARTERS // 2
    high = groups + groups // QUARTERS - low
    smem = pl.BlockSpec(memory_space=pltpu.SMEM)
    whole = pl.BlockSpec(memory_space=pltpu.VMEM)
    firsts = jnp.pad(first_labels, (0, LANES - first_width)).astype(jnp.float32)
    return pl.pallas_call(
        functools.partial(pack_kernel, folds),
        grid=(second_width // per_step,),
        in_specs=[
            smem,
            smem,
            pl.BlockSpec((per_step, first_width, slab), lambda i: (i, 0, 0)),
            whole,
            whole,
            pl.BlockSpec(memory_space=pl.ANY),
        ],
        out_specs=[whole, whole, whole],
        out_shape=[
            jax.ShapeDtypeStruct((low, LANES, LANES), jnp.bfloat16),
            jax.ShapeDtypeStruct((high, LANES, LANES), jnp.bfloat16),
            jax.ShapeDtypeStruct((1, slab), jnp.int32),
        ],
        scratch_shapes=[
            pltpu.VMEM((slab, 2 * LANES), jnp.bfloat16),
            pltpu.VMEM((pitch, LANES), jnp.float32),
            pltpu.VMEM((per_step * pitch, slab), jnp.bfloat16),
            pltpu.VMEM((per_step * pitch, LANES), jnp.float32),
            pltpu.VMEM((per_step * pitch, LANES), jnp.float32),
            pltpu.VMEM((groups * LANES, LANES), jnp.float32),
            pltpu.VMEM((groups * LANES, LANES), jnp.float32),
        ],
        compiler_params=pltpu.CompilerParams(
            dimension_semantics=("arbitrary",), vmem_limit_bytes=VMEM_LIMIT
        ),
        cost_estimate=pl.CostEstimate(
            flops=2 * 2600 * slab * 256, bytes_accessed=6_000_000, transcendentals=0
        ),
        name="pack_integrals",
    )(
        which,
        second_labels,
        jnp.transpose(integrals, (1, 0, 2)),
        firsts.reshape(1, LANES),
        slab_irrep.astype(jnp.float32).reshape(1, slab),
        after,
    )


def spread_kernel(
    folds, second_width, rest, parts, here_ref, amp_ref, out_ref,
    wide, strided, shifted, stage,
):
    virt = amp_ref.shape[1]
    tiles = wide.shape[0]
    tall = virt // folds
    last = (tiles - 1) * LANES
    early = iota((tall, LANES), 1) < LANES // 2
    for t in range(tiles):
        if t < tiles - 1:
            wide[t] = amp_ref[0, :, t * LANES : (t + 1) * LANES].astype(jnp.float32)
        else:
            wide[t] = jnp.zeros((virt, LANES), jnp.float32)
            wide[t, :, : virt - last] = amp_ref[0, :, last:].astype(jnp.float32)
    for f in range(folds):
        held = None
        for t in range(tiles):
            piece = wide[t, pl.ds(f, tall, stride=folds), :]
            strided[f, :, t * LANES : (t + 1) * LANES] = piece.astype(jnp.bfloat16)
            rolled = pltpu.roll(piece, LANES // 2, 1)
            if t > 0:
                shifted[f, :, (t - 1) * LANES : t * LANES] = jnp.where(
                    early, held, rolled
                ).astype(jnp.bfloat16)
            held = rolled
    span = 2 * second_width
    source = iota((LANES, 1), 0)
    lane = iota((LANES, 2 * LANES), 1)
    slots = rest // parts // 2
    for w in range(rest // 2):
        tile, offset = divmod(span * w, LANES)
        held = strided
        if offset + span > LANES:
            held, offset = shifted, offset - LANES // 2
        column = source - offset
        inside = (column >= 0) & (column < span)
        target = column + jnp.where(column >= second_width, LANES - second_width, 0)
        target = jnp.where(inside, target, -LANES)
        at = slice(tile * LANES, (tile + 1) * LANES)
        select = jnp.concatenate(
            [one_hot(lane == target + f * second_width) for f in range(folds)], axis=0
        )
        total = dot(jnp.concatenate([held[f, :, at] for f in range(folds)], axis=1), select)
        for a in range(2):
            outer, inner = divmod(2 * w + a, parts)
            away = lax.rem(outer - here_ref[0] + rest // parts, rest // parts)
            place = sum(jnp.where(away == k, AWAYS.index(k), 0) for k in AWAYS)
            half = place // slots
            stage[half, inner, pl.ds(place - half * slots, tall, stride=slots), :] = total[
                :, a * LANES : (a + 1) * LANES
            ]
    owners = out_ref.shape[1]
    rows = out_ref.shape[3] // 2
    for inner in range(parts):
        for i in range(owners):
            for half in range(2):
                out_ref[inner, i, 0, half * rows : (half + 1) * rows] = stage[
                    half, inner, i * rows : (i + 1) * rows, :
                ].astype(jnp.bfloat16)


def spread_amplitudes(here, amplitudes, owners, outer, parts):
    pairs, virt, _ = amplitudes.shape
    rest = outer * parts
    second_width = virt // rest
    folds = LANES // second_width
    tiles = -(-virt // LANES)
    tall = virt // folds
    rows = tall // owners * outer
    return pl.pallas_call(
        functools.partial(spread_kernel, folds, second_width, rest, parts),
        grid=(pairs,),
        in_specs=[
            pl.BlockSpec(memory_space=pltpu.SMEM),
            pl.BlockSpec((1, virt, virt), lambda p: (p, 0, 0)),
        ],
        out_specs=pl.BlockSpec((parts, owners, 1, rows, LANES), lambda p: (0, 0, p, 0, 0)),
        out_shape=jax.ShapeDtypeStruct((parts, owners, pairs, rows, LANES), jnp.bfloat16),
        scratch_shapes=[
            pltpu.VMEM((tiles, virt, LANES), jnp.float32),
            pltpu.VMEM((folds, tall, tiles * LANES), jnp.bfloat16),
            pltpu.VMEM((folds, tall, (tiles - 1) * LANES), jnp.bfloat16),
            pltpu.VMEM((2, parts, tall * outer // 2, LANES), jnp.float32),
        ],
        compiler_params=pltpu.CompilerParams(
            dimension_semantics=("arbitrary",), vmem_limit_bytes=VMEM_LIMIT
        ),
        cost_estimate=pl.CostEstimate(
            flops=2 * 480 * 80 * 65536, bytes_accessed=8_000_000, transcendentals=0
        ),
        name="spread_amplitudes",
    )(here, amplitudes)


def masked_rows(left, at, piece, label):
    tall = piece.shape[0]
    for g in range(IRREPS):
        left[g * tall : (g + 1) * tall, at : at + LANES] = piece * one_hot(label == g)


def contract_kernel(tile, slots, shards, half, amp_ref, labels_ref, *refs):
    refs = list(refs)
    first = half == 0
    start_ref = None if first else refs.pop(0)
    blocks = [(refs[2 * k], refs[2 * k + 1]) for k in range(shards)]
    refs = refs[2 * shards :]
    out_ref = refs.pop(0)
    rest_ref = refs.pop(0) if shards < slots else None
    (amps, labels, turned, left_a, left_b, right, spares, swap,
     amp_sems, block_sems, spare_sems, one_sems) = refs
    all_pairs = amps.shape[1]
    steps = amps.shape[0]
    groups = right.shape[0]
    per_quarter = groups // QUARTERS
    each = tile // slots
    square = tile * tile
    chunk = 2 * all_pairs

    def amp_copy(k):
        at = pl.ds(half * steps * tile + k * tile, tile)
        return pltpu.make_async_copy(amp_ref.at[:, at], amps.at[k], amp_sems.at[k])

    copies = []
    split, cut = groups // 2, per_quarter // 2
    for k, pair in enumerate(blocks):
        for h, block in enumerate(pair):
            copies.append(
                pltpu.make_async_copy(
                    block.at[pl.ds(0, split)],
                    right.at[pl.ds(h * split, split), k, :, pl.ds(0, LANES)],
                    block_sems.at[2 * k + h],
                )
            )
            count = (cut, per_quarter - cut)[h]
            copies.append(
                pltpu.make_async_copy(
                    block.at[pl.ds(split, count)],
                    spares.at[k, pl.ds(h * cut, count)],
                    spare_sems.at[2 * k + h],
                )
            )
    if not first:
        copies.append(pltpu.make_async_copy(start_ref, out_ref, one_sems.at[0]))
    labels_copy = pltpu.make_async_copy(labels_ref, labels, one_sems.at[1])
    amp_copies = [amp_copy(k) for k in range(steps)]
    amp_copies[0].start()
    labels_copy.start()
    for copy in copies:
        copy.start()
    for copy in amp_copies[1:]:
        copy.start()
    order = iota((square, square), 0)
    swap[...] = one_hot(iota((square, square), 1) == (order % tile) * tile + order // tile)
    quarter = iota((1, LANES), 1) // SPARE
    labels_copy.wait()

    def build(k, left):
        amp_copies[k].wait()
        for p in range(0, all_pairs, 2 * tile):
            pieces = [amps[k, q : q + tile].reshape(square, LANES) for q in (p, p + tile)]
            done = dot(swap[...], jnp.concatenate(pieces, axis=1)).astype(jnp.bfloat16)
            for r in range(tile):
                for h in range(2):
                    turned[k % 2, r, p + h * tile : p + (h + 1) * tile, :] = done[
                        r * tile : (r + 1) * tile, h * LANES : (h + 1) * LANES
                    ]
        for r in range(tile):
            group, slot = divmod(r, slots)
            if slot < shards:
                label = labels[k * tile + r : k * tile + r + 1, :]
                masked_rows(left, (group * shards + slot) * LANES, turned[k % 2, r], label)
            else:
                rest_ref[k * each + group] = turned[k % 2, r]

    lefts = (left_a, left_b)
    build(0, left_a)
    for copy in copies:
        copy.wait()
    for c in range(groups):
        keep = one_hot(quarter == c // per_quarter)
        for k in range(shards):
            right[c, k, :, LANES:] = spares[k, c % per_quarter] * keep
    for k in range(steps):
        if k + 1 < steps:
            build(k + 1, lefts[(k + 1) % 2])
        block = right[k * each : (k + 1) * each].reshape(each * shards * LANES, 2 * LANES)
        left = lefts[k % 2]
        for m in range(0, left.shape[0], chunk):
            product = dot(left[m : m + chunk], block)
            if first and k == 0:
                out_ref[m : m + chunk] = product
            else:
                out_ref[m : m + chunk] += product


def contract(amplitudes, labels, start, blocks, half):
    all_pairs, rows, _ = amplitudes.shape
    tile = 16
    slots = 4
    shards = len(blocks)
    groups = rows // (2 * slots)
    per_quarter = groups // QUARTERS
    whole = pl.BlockSpec(memory_space=pltpu.VMEM)
    hbm = pl.BlockSpec(memory_space=pl.ANY)
    steps = rows // 2 // tile
    tall = IRREPS * all_pairs
    wide = tile // slots * shards * LANES
    operands = (() if half == 0 else (start,)) + tuple(sum(blocks, ()))
    out_shape = [jax.ShapeDtypeStruct((tall, 2 * LANES), jnp.float32)]
    if shards < slots:
        out_shape.append(jax.ShapeDtypeStruct((groups, all_pairs, LANES), jnp.bfloat16))
    return pl.pallas_call(
        functools.partial(contract_kernel, tile, slots, shards, half),
        in_specs=[hbm] * (2 + len(operands)),
        out_specs=[whole] * len(out_shape),
        out_shape=out_shape,
        scratch_shapes=[
            pltpu.VMEM((steps, all_pairs, tile, LANES), jnp.bfloat16),
            pltpu.VMEM(labels.shape, labels.dtype),
            pltpu.VMEM((2, tile, all_pairs, LANES), jnp.bfloat16),
            pltpu.VMEM((tall, wide), jnp.bfloat16),
            pltpu.VMEM((tall, wide), jnp.bfloat16),
            pltpu.VMEM((groups, shards, LANES, 2 * LANES), jnp.bfloat16),
            pltpu.VMEM((shards, per_quarter, LANES, LANES), jnp.bfloat16),
            pltpu.VMEM((tile * tile, tile * tile), jnp.bfloat16),
            pltpu.SemaphoreType.DMA((steps,)),
            pltpu.SemaphoreType.DMA((2 * shards,)),
            pltpu.SemaphoreType.DMA((2 * shards,)),
            pltpu.SemaphoreType.DMA((2,)),
        ],
        compiler_params=pltpu.CompilerParams(vmem_limit_bytes=VMEM_LIMIT),
        cost_estimate=pl.CostEstimate(
            flops=2 * 768 * 10240 * 256, bytes_accessed=6_000_000, transcendentals=0
        ),
        name="contract",
    )(amplitudes, labels, *operands)


def last_kernel(pairs, slots, cores, core_ref, rest_hbm, labels_hbm, start_hbm, low_hbm, high_hbm,
                mine_ref, other_ref, rest, labels, start, left, right, spares, main, over, sems):
    groups, all_pairs, _ = rest.shape
    per_quarter = groups // QUARTERS
    split, cut = groups // 2, per_quarter // 2
    half = pl.ds(0, LANES)
    first = [
        pltpu.make_async_copy(rest_hbm, rest, sems.at[0]),
        pltpu.make_async_copy(labels_hbm, labels, sems.at[1]),
    ]
    second = [
        pltpu.make_async_copy(
            low_hbm.at[pl.ds(0, split)], right.at[pl.ds(0, split), :, half], sems.at[2]
        ),
        pltpu.make_async_copy(
            high_hbm.at[pl.ds(0, split)], right.at[pl.ds(split, split), :, half], sems.at[3]
        ),
        pltpu.make_async_copy(low_hbm.at[pl.ds(split, cut)], spares.at[pl.ds(0, cut)], sems.at[4]),
        pltpu.make_async_copy(
            high_hbm.at[pl.ds(split, per_quarter - cut)],
            spares.at[pl.ds(cut, per_quarter - cut)],
            sems.at[5],
        ),
    ]
    third = pltpu.make_async_copy(start_hbm, start, sems.at[6])
    for copy in first + second + [third]:
        copy.start()
    for copy in first:
        copy.wait()
    quarter = iota((1, LANES), 1) // SPARE
    for c in range(groups):
        row = c * slots + slots - 1
        masked_rows(left, c * LANES, rest[c], labels[row : row + 1, :])
    for copy in second:
        copy.wait()
    for c in range(groups):
        right[c, :, LANES:] = spares[c % per_quarter] * one_hot(quarter == c // per_quarter)
    product = dot(left[...], right[...].reshape(groups * LANES, 2 * LANES))
    third.wait()
    total = start[...] + product
    main[...] = total[:, :LANES]
    spare = total[:, LANES:]
    spare = spare + pltpu.roll(spare, 2 * SPARE, 1)
    over[...] = spare + pltpu.roll(spare, SPARE, 1)
    owners = all_pairs // pairs
    lines = mine_ref.shape[0] // (owners // cores)
    run = 8
    per = IRREPS // QUARTERS

    def emit(core, ref):
        ref[...] = jnp.zeros_like(ref)
        for block in range(owners // cores // run):
            owner = (block * cores + core) * run
            base = block * run * lines
            for g in range(IRREPS):
                for p in range(pairs):
                    at = g * all_pairs + owner * pairs + p
                    ref[pl.ds(base + g * pairs + p, run, stride=lines), :] = main[
                        pl.ds(at, run, stride=pairs), :
                    ]
            for g in range(per):
                for p in range(pairs):
                    value = jnp.zeros((run, LANES), jnp.float32)
                    for q in range(QUARTERS):
                        at = (q * per + g) * all_pairs + owner * pairs + p
                        piece = over[pl.ds(at, run, stride=pairs), :]
                        value = value + jnp.where(quarter == q, piece, 0.0)
                    at = base + (IRREPS + g) * pairs + p
                    ref[pl.ds(at, run, stride=lines), :] = value

    for core in range(cores):

        @pl.when(core_ref[0] == core)
        def _():
            emit(core, mine_ref)

        @pl.when(core_ref[0] != core)
        def _():
            emit(core, other_ref)


def contract_last(core, rest, labels, start, low, high, pairs):
    groups, all_pairs, _ = rest.shape
    cores = 2
    owners = all_pairs // pairs
    lines = -(-(IRREPS + IRREPS // QUARTERS) * pairs // 8) * 8
    whole = pl.BlockSpec(memory_space=pltpu.VMEM)
    hbm = pl.BlockSpec(memory_space=pl.ANY)
    tall = IRREPS * all_pairs
    shape = jax.ShapeDtypeStruct((owners // cores * lines, LANES), jnp.float32)
    return pl.pallas_call(
        functools.partial(last_kernel, pairs, labels.shape[0] // groups, cores),
        in_specs=[pl.BlockSpec(memory_space=pltpu.SMEM)] + [hbm] * 5,
        out_specs=[whole, whole],
        out_shape=[shape, shape],
        scratch_shapes=[
            pltpu.VMEM(rest.shape, rest.dtype),
            pltpu.VMEM(labels.shape, labels.dtype),
            pltpu.VMEM(start.shape, start.dtype),
            pltpu.VMEM((tall, groups * LANES), jnp.bfloat16),
            pltpu.VMEM((groups, LANES, 2 * LANES), jnp.bfloat16),
            pltpu.VMEM((groups // QUARTERS, LANES, LANES), jnp.bfloat16),
            pltpu.VMEM((tall, LANES), jnp.float32),
            pltpu.VMEM((tall, LANES), jnp.float32),
            pltpu.SemaphoreType.DMA((7,)),
        ],
        compiler_params=pltpu.CompilerParams(vmem_limit_bytes=VMEM_LIMIT),
        cost_estimate=pl.CostEstimate(
            flops=2 * 768 * 2560 * 256, bytes_accessed=3_000_000, transcendentals=0
        ),
        name="contract_last",
    )(core, rest, labels, start, low, high)


def unpack_kernel(pairs, round_ref, parts_ref, rank_ref, slab_ref, out_ref):
    rows = parts_ref.shape[1]
    slab = slab_ref.shape[1]
    summed = parts_ref[0]
    for k in range(1, parts_ref.shape[0]):
        summed = summed + parts_ref[k]
    irrep = slab_ref[...]
    rank = rank_ref[...] - round_ref[0] * CAP
    each = IRREPS // QUARTERS
    inside = (rank >= 0) & (rank < CAP)
    spare = rank >= LANES
    target = jnp.where(spare, (irrep // each) * SPARE + rank - LANES, rank)
    target = jnp.where(inside, target, -1)
    pick = jnp.where(iota((LANES, slab), 0) == target, 1.0, 0.0)
    values = jnp.dot(
        summed, pick, preferred_element_type=jnp.float32, precision=lax.Precision.HIGHEST
    )
    first = jnp.where(spare, (IRREPS + irrep % each) * pairs, irrep * pairs)
    row = iota((rows, slab), 0)
    for p in range(pairs):
        out_ref[p : p + 1, :] = jnp.sum(
            jnp.where(row == first + p, values, 0.0), axis=0, keepdims=True
        )


def unpack(which, parts, rank, slab_irrep, pairs):
    slab = slab_irrep.shape[0]
    whole = pl.BlockSpec(memory_space=pltpu.VMEM)
    return pl.pallas_call(
        functools.partial(unpack_kernel, pairs),
        in_specs=[pl.BlockSpec(memory_space=pltpu.SMEM), whole, whole, whole],
        out_specs=whole,
        out_shape=jax.ShapeDtypeStruct((pairs, slab), jnp.float32),
        compiler_params=pltpu.CompilerParams(vmem_limit_bytes=VMEM_LIMIT),
        name="unpack",
    )(which, parts, rank, slab_irrep.reshape(1, slab))


def local(amplitudes, integrals, virt_irrep, slab_irrep):
    pairs = amplitudes.shape[0]
    owners = lax.axis_size("va")
    count = lax.axis_size("vb")
    parts = lax.axis_size("occ")
    first_width, second_width, _ = integrals.shape
    folds = LANES // second_width
    groups = first_width // folds
    here = lax.axis_index("vb")
    part = lax.axis_index("occ")

    first_labels = lax.dynamic_slice_in_dim(
        virt_irrep, lax.axis_index("va") * first_width, first_width, 0
    )
    second_labels = lax.dynamic_index_in_dim(
        virt_irrep.reshape(count, parts, second_width), part, 1, keepdims=False
    )
    own_labels = lax.dynamic_index_in_dim(second_labels, here, 0, keepdims=False)
    order = lax.rem(here + jnp.array(AWAYS, jnp.int32), count)
    labels = jnp.bitwise_xor(
        first_labels.reshape(groups, 1, folds, 1),
        jnp.take(second_labels, order, axis=0).reshape(1, count, 1, second_width),
    ).reshape(groups, count, folds * second_width)
    labels = jnp.pad(
        labels, ((0, 0), (0, 0), (0, LANES - folds * second_width)), constant_values=-1
    )
    near_labels = labels[:, : count // 2].reshape(-1, LANES)
    far_labels = labels[:, count // 2 :].reshape(-1, LANES)

    up = [(i, (i + 1) % count) for i in range(count)]
    down = [(i, (i - 1) % count) for i in range(count)]

    same_core = [
        [(2 * k + core) * owners + i for k in range(parts // 2) for i in range(owners)]
        for core in range(2)
    ]

    def shifted(pair, perm):
        return tuple(lax.ppermute(block, "vb", perm) for block in pair)

    def blocks_of(which, after):
        low, high, rank = pack_integrals(
            which, integrals, first_labels, own_labels, slab_irrep, after
        )
        packed = low, high
        r1, l1 = shifted(packed, up), shifted(packed, down)
        r2, l2 = shifted(r1, up), shifted(l1, down)
        r3, l3 = shifted(r2, up), shifted(l2, down)
        return (packed, l1, r1, l2), (r2, r3, l3), rank

    def finish(which, near, middle, rank, arrived):
        (start,) = contract(arrived, near_labels, None, near, 0)
        up_end, down_end, start = lax.optimization_barrier((middle[1][0], middle[2][1], start))
        far = lax.ppermute(up_end, "vb", up), lax.ppermute(down_end, "vb", down)
        start, rest = contract(arrived, far_labels, start, middle, 1)
        core = lax.rem(part, 2)
        mine, other = contract_last(core.reshape(1), rest, far_labels, start, *far, pairs)
        partial = mine + lax.ppermute(other, "occ", [(i, i ^ 1) for i in range(parts)])
        partial = partial.reshape(parts // 2 * owners, -1, LANES)
        summands = lax.all_to_all(
            partial, SOURCES, split_axis=0, concat_axis=0, tiled=True, axis_index_groups=same_core
        )
        return unpack(which, summands, rank, slab_irrep, pairs)

    first = jnp.zeros((1,), jnp.int32)
    spread = spread_amplitudes(here.reshape(1), amplitudes, owners, count, parts)
    sent = spread.reshape((parts * owners,) + spread.shape[2:])
    arrived = lax.all_to_all(sent, SOURCES, split_axis=0, concat_axis=0, tiled=True)
    arrived = arrived.reshape((parts * owners * pairs,) + spread.shape[3:])
    near, middle, rank = blocks_of(first, spread)
    result = finish(first, near, middle, rank, arrived)
    largest = jnp.max(rank)

    def more(carry):
        return carry[0] * CAP <= largest

    def step(carry):
        which = carry[0].reshape(1)
        near, middle, rank = blocks_of(which, spread)
        return carry[0] + 1, carry[1] + finish(which, near, middle, rank, arrived)

    return lax.while_loop(more, step, (jnp.int32(1), result))[1]


def solution(mesh):
    return jax.shard_map(
        local,
        mesh=mesh,
        in_specs=(P(("va", "vb", "occ"), None, None), P("va", ("vb", "occ"), None), P(), P()),
        out_specs=P(("va", "vb", "occ"), None),
        check_vma=False,
    )
```

```python
import functools

import jax
import jax.numpy as jnp
from jax import lax
from jax.experimental import pallas as pl
from jax.experimental.pallas import tpu as pltpu
from jax.sharding import PartitionSpec as P

LANES = 128
IRREPS = 8
SPARE = 32
CAP = LANES + SPARE
QUARTERS = LANES // SPARE
MIB = 1024 * 1024
SOURCES = ("occ", "va")
AWAYS = (0, 1, 7, 2, 6, 5, 3, 4)


def iota(shape, axis):
    return lax.broadcasted_iota(jnp.int32, shape, axis)


def one_hot(hits):
    return jnp.where(hits, 1.0, 0.0).astype(jnp.bfloat16)


def dot(a, b):
    return jnp.dot(a, b, preferred_element_type=jnp.float32)


def pack_kernel(
    folds, round_ref, second_ref, block_ref, first_ref, row_ref, after_ref,
    low_ref, high_ref, rank_ref, onehot, firsts, masked, part_main, part_over, main, over,
):
    del after_ref
    step = pl.program_id(0)
    per_step, first_width, slab = block_ref.shape
    second_width = per_step * pl.num_programs(0)
    pitch = masked.shape[0] // per_step
    groups = first_width // folds
    square = (LANES, LANES)

    def turned(vector):
        return jnp.transpose(jnp.broadcast_to(vector, square))

    @pl.when(step == 0)
    def _():
        masked[...] = jnp.zeros_like(masked)
        for pad in range(folds * second_width, LANES):
            rows = pl.ds(pad, groups, stride=LANES)
            main[rows, :] = jnp.zeros((groups, LANES), jnp.float32)
            over[rows, :] = jnp.zeros((groups, LANES), jnp.float32)
        firsts[...] = turned(first_ref[...])[: firsts.shape[0]]
        offset = (round_ref[0] * CAP).astype(jnp.float32)
        before = one_hot(iota(square, 0) < iota(square, 1))
        lane = iota((LANES, 2 * LANES), 1).astype(jnp.float32)
        base = jnp.zeros((IRREPS, 1), jnp.float32)
        for k in range(slab // LANES):
            at = slice(k * LANES, (k + 1) * LANES)
            own = iota((IRREPS, LANES), 0).astype(jnp.float32) == row_ref[:, at]
            member = jnp.where(own, 1.0, 0.0)
            count = dot(member.astype(jnp.bfloat16), before) + base
            rank = jnp.sum(jnp.where(own, count, 0.0), axis=0, keepdims=True)
            rank_ref[:, at] = rank.astype(jnp.int32)
            base = base + jnp.sum(member, axis=1, keepdims=True)
            column = turned(rank) - offset
            onehot[at, :] = one_hot(lane == jnp.concatenate([column, column], axis=1))

    for k in range(per_step):
        second = second_ref[step * per_step + k]
        wanted = jnp.bitwise_xor(firsts[...].astype(jnp.int32), second).astype(jnp.float32)
        wanted = wanted[:first_width]
        for t in range(slab // LANES):
            at = slice(t * LANES, (t + 1) * LANES)
            allowed = wanted == row_ref[:, at]
            values = jnp.where(allowed, block_ref[k, :, at].astype(jnp.float32), 0.0)
            masked[k * pitch : k * pitch + first_width, at] = values.astype(jnp.bfloat16)
    packed = dot(masked[...], onehot[...])
    part_main[...] = packed[:, :LANES]
    part_over[...] = packed[:, LANES:]
    for k in range(per_step):
        d = step * per_step + k
        for f in range(folds):
            source = pl.ds(k * pitch + f, groups, stride=folds)
            target = pl.ds(f * second_width + d, groups, stride=LANES)
            main[target, :] = part_main[source, :]
            over[target, :] = part_over[source, :]

    @pl.when(step == pl.num_programs(0) - 1)
    def _():
        per_quarter = groups // QUARTERS
        low = iota(square, 1) < SPARE
        split = groups // 2
        for e in range(per_quarter):
            spare = jnp.zeros(square, jnp.float32)
            for q in range(QUARTERS):
                group = q * per_quarter + e
                rows = slice(group * LANES, (group + 1) * LANES)
                packed = main[rows, :].astype(jnp.bfloat16)
                if group < split:
                    low_ref[group] = packed
                else:
                    high_ref[group - split] = packed
                piece = jnp.where(low, over[rows, :], 0.0)
                spare = spare + (piece if q == 0 else pltpu.roll(piece, q * SPARE, 1))
            spare = spare.astype(jnp.bfloat16)
            if e < per_quarter // 2:
                low_ref[split + e] = spare
            else:
                high_ref[split + e - per_quarter // 2] = spare


def pack_integrals(which, integrals, first_labels, second_labels, slab_irrep, after):
    first_width, second_width, slab = integrals.shape
    folds = LANES // second_width
    groups = first_width // folds
    per_step = 5
    pitch = -(-first_width // 16) * 16
    low = groups // 2 + groups // QUARTERS // 2
    high = groups + groups // QUARTERS - low
    smem = pl.BlockSpec(memory_space=pltpu.SMEM)
    whole = pl.BlockSpec(memory_space=pltpu.VMEM)
    firsts = jnp.pad(first_labels, (0, LANES - first_width)).astype(jnp.float32)
    return pl.pallas_call(
        functools.partial(pack_kernel, folds),
        grid=(second_width // per_step,),
        in_specs=[
            smem,
            smem,
            pl.BlockSpec((per_step, first_width, slab), lambda i: (i, 0, 0)),
            whole,
            whole,
            pl.BlockSpec(memory_space=pl.ANY),
        ],
        out_specs=[whole, whole, whole],
        out_shape=[
            jax.ShapeDtypeStruct((low, LANES, LANES), jnp.bfloat16),
            jax.ShapeDtypeStruct((high, LANES, LANES), jnp.bfloat16),
            jax.ShapeDtypeStruct((1, slab), jnp.int32),
        ],
        scratch_shapes=[
            pltpu.VMEM((slab, 2 * LANES), jnp.bfloat16),
            pltpu.VMEM((pitch, LANES), jnp.float32),
            pltpu.VMEM((per_step * pitch, slab), jnp.bfloat16),
            pltpu.VMEM((per_step * pitch, LANES), jnp.float32),
            pltpu.VMEM((per_step * pitch, LANES), jnp.float32),
            pltpu.VMEM((groups * LANES, LANES), jnp.float32),
            pltpu.VMEM((groups * LANES, LANES), jnp.float32),
        ],
        compiler_params=pltpu.CompilerParams(
            dimension_semantics=("arbitrary",), vmem_limit_bytes=16 * MIB
        ),
        cost_estimate=pl.CostEstimate(
            flops=2 * 2600 * slab * 256, bytes_accessed=6_000_000, transcendentals=0
        ),
        name="pack_integrals",
    )(
        which,
        second_labels,
        jnp.transpose(integrals, (1, 0, 2)),
        firsts.reshape(1, LANES),
        slab_irrep.astype(jnp.float32).reshape(1, slab),
        after,
    )


def spread_kernel(
    folds, second_width, rest, parts, here_ref, amp_ref, out_ref,
    wide, strided, shifted, stage,
):
    virt = amp_ref.shape[1]
    tiles = wide.shape[0]
    tall = virt // folds
    last = (tiles - 1) * LANES
    early = iota((tall, LANES), 1) < LANES // 2
    for t in range(tiles):
        if t < tiles - 1:
            wide[t] = amp_ref[0, :, t * LANES : (t + 1) * LANES].astype(jnp.float32)
        else:
            wide[t] = jnp.zeros((virt, LANES), jnp.float32)
            wide[t, :, : virt - last] = amp_ref[0, :, last:].astype(jnp.float32)
    for f in range(folds):
        held = None
        for t in range(tiles):
            piece = wide[t, pl.ds(f, tall, stride=folds), :]
            strided[f, :, t * LANES : (t + 1) * LANES] = piece.astype(jnp.bfloat16)
            rolled = pltpu.roll(piece, LANES // 2, 1)
            if t > 0:
                shifted[f, :, (t - 1) * LANES : t * LANES] = jnp.where(
                    early, held, rolled
                ).astype(jnp.bfloat16)
            held = rolled
    span = 2 * second_width
    source = iota((LANES, 1), 0)
    lane = iota((LANES, 2 * LANES), 1)
    slots = rest // parts // 2
    for w in range(rest // 2):
        tile, offset = divmod(span * w, LANES)
        held = strided
        if offset + span > LANES:
            held, offset = shifted, offset - LANES // 2
        column = source - offset
        inside = (column >= 0) & (column < span)
        target = column + jnp.where(column >= second_width, LANES - second_width, 0)
        target = jnp.where(inside, target, -LANES)
        at = slice(tile * LANES, (tile + 1) * LANES)
        select = jnp.concatenate(
            [one_hot(lane == target + f * second_width) for f in range(folds)], axis=0
        )
        total = dot(jnp.concatenate([held[f, :, at] for f in range(folds)], axis=1), select)
        for a in range(2):
            outer, inner = divmod(2 * w + a, parts)
            away = lax.rem(outer - here_ref[0] + rest // parts, rest // parts)
            place = sum(jnp.where(away == k, AWAYS.index(k), 0) for k in AWAYS)
            half = place // slots
            stage[half, inner, pl.ds(place - half * slots, tall, stride=slots), :] = total[
                :, a * LANES : (a + 1) * LANES
            ]
    owners = out_ref.shape[1]
    rows = out_ref.shape[3] // 2
    for inner in range(parts):
        for i in range(owners):
            for half in range(2):
                out_ref[inner, i, 0, half * rows : (half + 1) * rows] = stage[
                    half, inner, i * rows : (i + 1) * rows, :
                ].astype(jnp.bfloat16)


def spread_amplitudes(here, amplitudes, owners, outer, parts):
    pairs, virt, _ = amplitudes.shape
    rest = outer * parts
    second_width = virt // rest
    folds = LANES // second_width
    tiles = -(-virt // LANES)
    tall = virt // folds
    rows = tall // owners * outer
    return pl.pallas_call(
        functools.partial(spread_kernel, folds, second_width, rest, parts),
        grid=(pairs,),
        in_specs=[
            pl.BlockSpec(memory_space=pltpu.SMEM),
            pl.BlockSpec((1, virt, virt), lambda p: (p, 0, 0)),
        ],
        out_specs=pl.BlockSpec((parts, owners, 1, rows, LANES), lambda p: (0, 0, p, 0, 0)),
        out_shape=jax.ShapeDtypeStruct((parts, owners, pairs, rows, LANES), jnp.bfloat16),
        scratch_shapes=[
            pltpu.VMEM((tiles, virt, LANES), jnp.float32),
            pltpu.VMEM((folds, tall, tiles * LANES), jnp.bfloat16),
            pltpu.VMEM((folds, tall, (tiles - 1) * LANES), jnp.bfloat16),
            pltpu.VMEM((2, parts, tall * outer // 2, LANES), jnp.float32),
        ],
        compiler_params=pltpu.CompilerParams(
            dimension_semantics=("arbitrary",), vmem_limit_bytes=24 * MIB
        ),
        cost_estimate=pl.CostEstimate(
            flops=2 * 480 * 80 * 65536, bytes_accessed=8_000_000, transcendentals=0
        ),
        name="spread_amplitudes",
    )(here, amplitudes)


def masked_rows(left, at, piece, label):
    tall = piece.shape[0]
    for g in range(IRREPS):
        left[g * tall : (g + 1) * tall, at : at + LANES] = piece * one_hot(label == g)


def contract_kernel(tile, slots, shards, half, amp_ref, labels_ref, *refs):
    refs = list(refs)
    first = half == 0
    start_ref = None if first else refs.pop(0)
    blocks = [(refs[2 * k], refs[2 * k + 1]) for k in range(shards)]
    refs = refs[2 * shards :]
    out_ref = refs.pop(0)
    rest_ref = refs.pop(0) if shards < slots else None
    (amps, labels, turned, left_a, left_b, right, spares, swap,
     amp_sems, block_sems, spare_sems, one_sems) = refs
    all_pairs = amps.shape[1]
    steps = amps.shape[0]
    groups = right.shape[0]
    per_quarter = groups // QUARTERS
    each = tile // slots
    square = tile * tile
    chunk = 2 * all_pairs

    def amp_copy(k):
        at = pl.ds(half * steps * tile + k * tile, tile)
        return pltpu.make_async_copy(amp_ref.at[:, at], amps.at[k], amp_sems.at[k])

    copies = []
    split, cut = groups // 2, per_quarter // 2
    for k, pair in enumerate(blocks):
        for h, block in enumerate(pair):
            copies.append(
                pltpu.make_async_copy(
                    block.at[pl.ds(0, split)],
                    right.at[pl.ds(h * split, split), k, :, pl.ds(0, LANES)],
                    block_sems.at[2 * k + h],
                )
            )
            count = (cut, per_quarter - cut)[h]
            copies.append(
                pltpu.make_async_copy(
                    block.at[pl.ds(split, count)],
                    spares.at[k, pl.ds(h * cut, count)],
                    spare_sems.at[2 * k + h],
                )
            )
    if not first:
        copies.append(pltpu.make_async_copy(start_ref, out_ref, one_sems.at[0]))
    labels_copy = pltpu.make_async_copy(labels_ref, labels, one_sems.at[1])
    amp_copies = [amp_copy(k) for k in range(steps)]
    amp_copies[0].start()
    labels_copy.start()
    for copy in copies:
        copy.start()
    for copy in amp_copies[1:]:
        copy.start()
    order = iota((square, square), 0)
    swap[...] = one_hot(iota((square, square), 1) == (order % tile) * tile + order // tile)
    quarter = iota((1, LANES), 1) // SPARE
    labels_copy.wait()

    def build(k, left):
        amp_copies[k].wait()
        for p in range(0, all_pairs, 2 * tile):
            pieces = [amps[k, q : q + tile].reshape(square, LANES) for q in (p, p + tile)]
            done = dot(swap[...], jnp.concatenate(pieces, axis=1)).astype(jnp.bfloat16)
            for r in range(tile):
                for h in range(2):
                    turned[k % 2, r, p + h * tile : p + (h + 1) * tile, :] = done[
                        r * tile : (r + 1) * tile, h * LANES : (h + 1) * LANES
                    ]
        for r in range(tile):
            group, slot = divmod(r, slots)
            if slot < shards:
                label = labels[k * tile + r : k * tile + r + 1, :]
                masked_rows(left, (group * shards + slot) * LANES, turned[k % 2, r], label)
            else:
                rest_ref[k * each + group] = turned[k % 2, r]

    lefts = (left_a, left_b)
    build(0, left_a)
    for copy in copies:
        copy.wait()
    for c in range(groups):
        keep = one_hot(quarter == c // per_quarter)
        for k in range(shards):
            right[c, k, :, LANES:] = spares[k, c % per_quarter] * keep
    for k in range(steps):
        if k + 1 < steps:
            build(k + 1, lefts[(k + 1) % 2])
        block = right[k * each : (k + 1) * each].reshape(each * shards * LANES, 2 * LANES)
        left = lefts[k % 2]
        for m in range(0, left.shape[0], chunk):
            product = dot(left[m : m + chunk], block)
            if first and k == 0:
                out_ref[m : m + chunk] = product
            else:
                out_ref[m : m + chunk] += product


def contract(amplitudes, labels, start, blocks, half):
    all_pairs, rows, _ = amplitudes.shape
    tile = 16
    slots = 4
    shards = len(blocks)
    groups = rows // (2 * slots)
    per_quarter = groups // QUARTERS
    whole = pl.BlockSpec(memory_space=pltpu.VMEM)
    hbm = pl.BlockSpec(memory_space=pl.ANY)
    steps = rows // 2 // tile
    tall = IRREPS * all_pairs
    wide = tile // slots * shards * LANES
    operands = (() if half == 0 else (start,)) + tuple(sum(blocks, ()))
    out_shape = [jax.ShapeDtypeStruct((tall, 2 * LANES), jnp.float32)]
    if shards < slots:
        out_shape.append(jax.ShapeDtypeStruct((groups, all_pairs, LANES), jnp.bfloat16))
    return pl.pallas_call(
        functools.partial(contract_kernel, tile, slots, shards, half),
        in_specs=[hbm] * (2 + len(operands)),
        out_specs=[whole] * len(out_shape),
        out_shape=out_shape,
        scratch_shapes=[
            pltpu.VMEM((steps, all_pairs, tile, LANES), jnp.bfloat16),
            pltpu.VMEM(labels.shape, labels.dtype),
            pltpu.VMEM((2, tile, all_pairs, LANES), jnp.bfloat16),
            pltpu.VMEM((tall, wide), jnp.bfloat16),
            pltpu.VMEM((tall, wide), jnp.bfloat16),
            pltpu.VMEM((groups, shards, LANES, 2 * LANES), jnp.bfloat16),
            pltpu.VMEM((shards, per_quarter, LANES, LANES), jnp.bfloat16),
            pltpu.VMEM((tile * tile, tile * tile), jnp.bfloat16),
            pltpu.SemaphoreType.DMA((steps,)),
            pltpu.SemaphoreType.DMA((2 * shards,)),
            pltpu.SemaphoreType.DMA((2 * shards,)),
            pltpu.SemaphoreType.DMA((2,)),
        ],
        compiler_params=pltpu.CompilerParams(vmem_limit_bytes=26 * MIB),
        cost_estimate=pl.CostEstimate(
            flops=2 * 768 * 10240 * 256, bytes_accessed=6_000_000, transcendentals=0
        ),
        name="contract",
    )(amplitudes, labels, *operands)


def last_kernel(pairs, slots, cores, core_ref, rest_hbm, labels_hbm, start_hbm, low_hbm, high_hbm,
                mine_ref, other_ref, rest, labels, start, left, right, spares, main, over, sems):
    groups, all_pairs, _ = rest.shape
    per_quarter = groups // QUARTERS
    split, cut = groups // 2, per_quarter // 2
    half = pl.ds(0, LANES)
    first = [
        pltpu.make_async_copy(rest_hbm, rest, sems.at[0]),
        pltpu.make_async_copy(labels_hbm, labels, sems.at[1]),
    ]
    second = [
        pltpu.make_async_copy(
            low_hbm.at[pl.ds(0, split)], right.at[pl.ds(0, split), :, half], sems.at[2]
        ),
        pltpu.make_async_copy(
            high_hbm.at[pl.ds(0, split)], right.at[pl.ds(split, split), :, half], sems.at[3]
        ),
        pltpu.make_async_copy(low_hbm.at[pl.ds(split, cut)], spares.at[pl.ds(0, cut)], sems.at[4]),
        pltpu.make_async_copy(
            high_hbm.at[pl.ds(split, per_quarter - cut)],
            spares.at[pl.ds(cut, per_quarter - cut)],
            sems.at[5],
        ),
    ]
    third = pltpu.make_async_copy(start_hbm, start, sems.at[6])
    for copy in first + second + [third]:
        copy.start()
    for copy in first:
        copy.wait()
    quarter = iota((1, LANES), 1) // SPARE
    for c in range(groups):
        row = c * slots + slots - 1
        masked_rows(left, c * LANES, rest[c], labels[row : row + 1, :])
    for copy in second:
        copy.wait()
    for c in range(groups):
        right[c, :, LANES:] = spares[c % per_quarter] * one_hot(quarter == c // per_quarter)
    product = dot(left[...], right[...].reshape(groups * LANES, 2 * LANES))
    third.wait()
    total = start[...] + product
    main[...] = total[:, :LANES]
    spare = total[:, LANES:]
    spare = spare + pltpu.roll(spare, 2 * SPARE, 1)
    over[...] = spare + pltpu.roll(spare, SPARE, 1)
    owners = all_pairs // pairs
    lines = mine_ref.shape[0] // (owners // cores)
    run = 8
    per = IRREPS // QUARTERS

    def emit(core, ref):
        ref[...] = jnp.zeros_like(ref)
        for block in range(owners // cores // run):
            owner = (block * cores + core) * run
            base = block * run * lines
            for g in range(IRREPS):
                for p in range(pairs):
                    at = g * all_pairs + owner * pairs + p
                    ref[pl.ds(base + g * pairs + p, run, stride=lines), :] = main[
                        pl.ds(at, run, stride=pairs), :
                    ]
            for g in range(per):
                for p in range(pairs):
                    value = jnp.zeros((run, LANES), jnp.float32)
                    for q in range(QUARTERS):
                        at = (q * per + g) * all_pairs + owner * pairs + p
                        piece = over[pl.ds(at, run, stride=pairs), :]
                        value = value + jnp.where(quarter == q, piece, 0.0)
                    at = base + (IRREPS + g) * pairs + p
                    ref[pl.ds(at, run, stride=lines), :] = value

    for core in range(cores):

        @pl.when(core_ref[0] == core)
        def _():
            emit(core, mine_ref)

        @pl.when(core_ref[0] != core)
        def _():
            emit(core, other_ref)


def contract_last(core, rest, labels, start, low, high, pairs):
    groups, all_pairs, _ = rest.shape
    cores = 2
    owners = all_pairs // pairs
    lines = -(-(IRREPS + IRREPS // QUARTERS) * pairs // 8) * 8
    whole = pl.BlockSpec(memory_space=pltpu.VMEM)
    hbm = pl.BlockSpec(memory_space=pl.ANY)
    tall = IRREPS * all_pairs
    shape = jax.ShapeDtypeStruct((owners // cores * lines, LANES), jnp.float32)
    return pl.pallas_call(
        functools.partial(last_kernel, pairs, labels.shape[0] // groups, cores),
        in_specs=[pl.BlockSpec(memory_space=pltpu.SMEM)] + [hbm] * 5,
        out_specs=[whole, whole],
        out_shape=[shape, shape],
        scratch_shapes=[
            pltpu.VMEM(rest.shape, rest.dtype),
            pltpu.VMEM(labels.shape, labels.dtype),
            pltpu.VMEM(start.shape, start.dtype),
            pltpu.VMEM((tall, groups * LANES), jnp.bfloat16),
            pltpu.VMEM((groups, LANES, 2 * LANES), jnp.bfloat16),
            pltpu.VMEM((groups // QUARTERS, LANES, LANES), jnp.bfloat16),
            pltpu.VMEM((tall, LANES), jnp.float32),
            pltpu.VMEM((tall, LANES), jnp.float32),
            pltpu.SemaphoreType.DMA((7,)),
        ],
        compiler_params=pltpu.CompilerParams(vmem_limit_bytes=18 * MIB),
        cost_estimate=pl.CostEstimate(
            flops=2 * 768 * 2560 * 256, bytes_accessed=3_000_000, transcendentals=0
        ),
        name="contract_last",
    )(core, rest, labels, start, low, high)


def unpack_kernel(pairs, round_ref, parts_ref, rank_ref, slab_ref, rest_ref, out_ref):
    rows = parts_ref.shape[1]
    slab = slab_ref.shape[1]
    summed = parts_ref[0]
    for k in range(1, parts_ref.shape[0]):
        summed = summed + parts_ref[k]
    irrep = slab_ref[...]
    rank = rank_ref[...] - round_ref[0] * CAP
    each = IRREPS // QUARTERS
    inside = (rank >= 0) & (rank < CAP)
    spare = rank >= LANES
    target = jnp.where(spare, (irrep // each) * SPARE + rank - LANES, rank)
    target = jnp.where(inside, target, -1)
    pick = jnp.where(iota((LANES, slab), 0) == target, 1.0, 0.0)
    values = jnp.dot(
        summed, pick, preferred_element_type=jnp.float32, precision=lax.Precision.HIGHEST
    )
    first = jnp.where(spare, (IRREPS + irrep % each) * pairs, irrep * pairs)
    row = iota((rows, slab), 0)
    for p in range(pairs):
        out_ref[p : p + 1, :] = rest_ref[p : p + 1, :] + jnp.sum(
            jnp.where(row == first + p, values, 0.0), axis=0, keepdims=True
        )


def unpack(which, parts, rank, slab_irrep, rest):
    pairs, slab = rest.shape
    whole = pl.BlockSpec(memory_space=pltpu.VMEM)
    return pl.pallas_call(
        functools.partial(unpack_kernel, pairs),
        in_specs=[pl.BlockSpec(memory_space=pltpu.SMEM), whole, whole, whole, whole],
        out_specs=whole,
        out_shape=jax.ShapeDtypeStruct((pairs, slab), jnp.float32),
        compiler_params=pltpu.CompilerParams(vmem_limit_bytes=6 * MIB),
        name="unpack",
    )(which, parts, rank, slab_irrep.reshape(1, slab), rest)


def local(amplitudes, integrals, virt_irrep, slab_irrep):
    pairs = amplitudes.shape[0]
    owners = lax.axis_size("va")
    count = lax.axis_size("vb")
    parts = lax.axis_size("occ")
    first_width, second_width, _ = integrals.shape
    folds = LANES // second_width
    groups = first_width // folds
    here = lax.axis_index("vb")
    part = lax.axis_index("occ")

    first_labels = lax.dynamic_slice_in_dim(
        virt_irrep, lax.axis_index("va") * first_width, first_width, 0
    )
    second_labels = lax.dynamic_index_in_dim(
        virt_irrep.reshape(count, parts, second_width), part, 1, keepdims=False
    )
    own_labels = lax.dynamic_index_in_dim(second_labels, here, 0, keepdims=False)
    order = lax.rem(here + jnp.array(AWAYS, jnp.int32), count)
    labels = jnp.bitwise_xor(
        first_labels.reshape(groups, 1, folds, 1),
        jnp.take(second_labels, order, axis=0).reshape(1, count, 1, second_width),
    ).reshape(groups, count, folds * second_width)
    labels = jnp.pad(
        labels, ((0, 0), (0, 0), (0, LANES - folds * second_width)), constant_values=-1
    )
    near_labels = labels[:, : count // 2].reshape(-1, LANES)
    far_labels = labels[:, count // 2 :].reshape(-1, LANES)

    up = [(i, (i + 1) % count) for i in range(count)]
    down = [(i, (i - 1) % count) for i in range(count)]

    same_core = [
        [(2 * k + core) * owners + i for k in range(parts // 2) for i in range(owners)]
        for core in range(2)
    ]

    def shifted(pair, perm):
        return tuple(lax.ppermute(block, "vb", perm) for block in pair)

    def blocks_of(which, after):
        low, high, rank = pack_integrals(
            which, integrals, first_labels, own_labels, slab_irrep, after
        )
        packed = low, high
        r1, l1 = shifted(packed, up), shifted(packed, down)
        r2, l2 = shifted(r1, up), shifted(l1, down)
        r3, l3 = shifted(r2, up), shifted(l2, down)
        return (packed, l1, r1, l2), (r2, r3, l3), rank

    def finish(which, near, middle, rank, arrived, rest_of_sum):
        (start,) = contract(arrived, near_labels, None, near, 0)
        up_end, down_end, start = lax.optimization_barrier((middle[1][0], middle[2][1], start))
        far = lax.ppermute(up_end, "vb", up), lax.ppermute(down_end, "vb", down)
        start, rest = contract(arrived, far_labels, start, middle, 1)
        core = lax.rem(part, 2)
        mine, other = contract_last(core.reshape(1), rest, far_labels, start, *far, pairs)
        partial = mine + lax.ppermute(other, "occ", [(i, i ^ 1) for i in range(parts)])
        partial = partial.reshape(parts // 2 * owners, -1, LANES)
        summands = lax.all_to_all(
            partial, SOURCES, split_axis=0, concat_axis=0, tiled=True, axis_index_groups=same_core
        )
        return unpack(which, summands, rank, slab_irrep, rest_of_sum)

    first = jnp.zeros((1,), jnp.int32)
    spread = spread_amplitudes(here.reshape(1), amplitudes, owners, count, parts)
    sent = spread.reshape((parts * owners,) + spread.shape[2:])
    arrived = lax.all_to_all(sent, SOURCES, split_axis=0, concat_axis=0, tiled=True)
    arrived = arrived.reshape((parts * owners * pairs,) + spread.shape[3:])
    near, middle, rank = blocks_of(first, spread)
    largest = jnp.max(rank)

    def more(carry):
        return carry[0] * CAP <= largest

    def step(carry):
        which = carry[0].reshape(1)
        near, middle, rank = blocks_of(which, spread)
        return carry[0] + 1, finish(which, near, middle, rank, arrived, carry[1])

    nothing = jnp.zeros((pairs, slab_irrep.shape[0]), jnp.float32)
    later = lax.while_loop(more, step, (jnp.int32(1), nothing))[1]
    return finish(first, near, middle, rank, arrived, later)


def solution(mesh):
    return jax.shard_map(
        local,
        mesh=mesh,
        in_specs=(P(("va", "vb", "occ"), None, None), P("va", ("vb", "occ"), None), P(), P()),
        out_specs=P(("va", "vb", "occ"), None),
        check_vma=False,
    )
```

```python
import functools

import jax
import jax.numpy as jnp
from jax import lax
from jax.experimental import pallas as pl
from jax.experimental.pallas import tpu as pltpu
from jax.sharding import PartitionSpec as P

LANES = 128
IRREPS = 8
SPARE = 32
CAP = LANES + SPARE
QUARTERS = LANES // SPARE
MIB = 1024 * 1024
SOURCES = ("occ", "va")
AWAYS = (0, 1, 7, 2, 6, 5, 3, 4)


def iota(shape, axis):
    return lax.broadcasted_iota(jnp.int32, shape, axis)


def one_hot(hits):
    return jnp.where(hits, 1.0, 0.0).astype(jnp.bfloat16)


def dot(a, b):
    return jnp.dot(a, b, preferred_element_type=jnp.float32)


def pack_kernel(
    folds, round_ref, second_ref, block_ref, first_ref, row_ref, after_ref,
    low_ref, high_ref, rank_ref, onehot, firsts, masked, part_main, part_over, main, over,
):
    del after_ref
    step = pl.program_id(0)
    per_step, first_width, slab = block_ref.shape
    second_width = per_step * pl.num_programs(0)
    pitch = masked.shape[0] // per_step
    groups = first_width // folds
    square = (LANES, LANES)

    def turned(vector):
        return jnp.transpose(jnp.broadcast_to(vector, square))

    @pl.when(step == 0)
    def _():
        masked[...] = jnp.zeros_like(masked)
        for pad in range(folds * second_width, LANES):
            rows = pl.ds(pad, groups, stride=LANES)
            main[rows, :] = jnp.zeros((groups, LANES), jnp.float32)
            over[rows, :] = jnp.zeros((groups, LANES), jnp.float32)
        firsts[...] = turned(first_ref[...])[: firsts.shape[0]]
        offset = (round_ref[0] * CAP).astype(jnp.float32)
        before = one_hot(iota(square, 0) < iota(square, 1))
        lane = iota((LANES, 2 * LANES), 1).astype(jnp.float32)
        base = jnp.zeros((IRREPS, 1), jnp.float32)
        for k in range(slab // LANES):
            at = slice(k * LANES, (k + 1) * LANES)
            own = iota((IRREPS, LANES), 0).astype(jnp.float32) == row_ref[:, at]
            member = jnp.where(own, 1.0, 0.0)
            count = dot(member.astype(jnp.bfloat16), before) + base
            rank = jnp.sum(jnp.where(own, count, 0.0), axis=0, keepdims=True)
            rank_ref[:, at] = rank.astype(jnp.int32)
            base = base + jnp.sum(member, axis=1, keepdims=True)
            column = turned(rank) - offset
            onehot[at, :] = one_hot(lane == jnp.concatenate([column, column], axis=1))

    for k in range(per_step):
        second = second_ref[step * per_step + k]
        wanted = jnp.bitwise_xor(firsts[...].astype(jnp.int32), second).astype(jnp.float32)
        wanted = wanted[:first_width]
        for t in range(slab // LANES):
            at = slice(t * LANES, (t + 1) * LANES)
            allowed = wanted == row_ref[:, at]
            values = jnp.where(allowed, block_ref[k, :, at].astype(jnp.float32), 0.0)
            masked[k * pitch : k * pitch + first_width, at] = values.astype(jnp.bfloat16)
    packed = dot(masked[...], onehot[...])
    part_main[...] = packed[:, :LANES]
    part_over[...] = packed[:, LANES:]
    for k in range(per_step):
        d = step * per_step + k
        for f in range(folds):
            source = pl.ds(k * pitch + f, groups, stride=folds)
            target = pl.ds(f * second_width + d, groups, stride=LANES)
            main[target, :] = part_main[source, :]
            over[target, :] = part_over[source, :]

    @pl.when(step == pl.num_programs(0) - 1)
    def _():
        per_quarter = groups // QUARTERS
        low = iota(square, 1) < SPARE
        split = groups // 2
        for e in range(per_quarter):
            spare = jnp.zeros(square, jnp.float32)
            for q in range(QUARTERS):
                group = q * per_quarter + e
                rows = slice(group * LANES, (group + 1) * LANES)
                packed = main[rows, :].astype(jnp.bfloat16)
                if group < split:
                    low_ref[group] = packed
                else:
                    high_ref[group - split] = packed
                piece = jnp.where(low, over[rows, :], 0.0)
                spare = spare + (piece if q == 0 else pltpu.roll(piece, q * SPARE, 1))
            spare = spare.astype(jnp.bfloat16)
            if e < per_quarter // 2:
                low_ref[split + e] = spare
            else:
                high_ref[split + e - per_quarter // 2] = spare


def pack_integrals(which, integrals, first_labels, second_labels, slab_irrep, after):
    first_width, second_width, slab = integrals.shape
    folds = LANES // second_width
    groups = first_width // folds
    per_step = 5
    pitch = -(-first_width // 16) * 16
    low = groups // 2 + groups // QUARTERS // 2
    high = groups + groups // QUARTERS - low
    smem = pl.BlockSpec(memory_space=pltpu.SMEM)
    whole = pl.BlockSpec(memory_space=pltpu.VMEM)
    firsts = jnp.pad(first_labels, (0, LANES - first_width)).astype(jnp.float32)
    return pl.pallas_call(
        functools.partial(pack_kernel, folds),
        grid=(second_width // per_step,),
        in_specs=[
            smem,
            smem,
            pl.BlockSpec((per_step, first_width, slab), lambda i: (i, 0, 0)),
            whole,
            whole,
            pl.BlockSpec(memory_space=pl.ANY),
        ],
        out_specs=[whole, whole, whole],
        out_shape=[
            jax.ShapeDtypeStruct((low, LANES, LANES), jnp.bfloat16),
            jax.ShapeDtypeStruct((high, LANES, LANES), jnp.bfloat16),
            jax.ShapeDtypeStruct((1, slab), jnp.int32),
        ],
        scratch_shapes=[
            pltpu.VMEM((slab, 2 * LANES), jnp.bfloat16),
            pltpu.VMEM((pitch, LANES), jnp.float32),
            pltpu.VMEM((per_step * pitch, slab), jnp.bfloat16),
            pltpu.VMEM((per_step * pitch, LANES), jnp.float32),
            pltpu.VMEM((per_step * pitch, LANES), jnp.float32),
            pltpu.VMEM((groups * LANES, LANES), jnp.float32),
            pltpu.VMEM((groups * LANES, LANES), jnp.float32),
        ],
        compiler_params=pltpu.CompilerParams(
            dimension_semantics=("arbitrary",), vmem_limit_bytes=16 * MIB
        ),
        cost_estimate=pl.CostEstimate(
            flops=2 * 2600 * slab * 256, bytes_accessed=6_000_000, transcendentals=0
        ),
        name="pack_integrals",
    )(
        which,
        second_labels,
        jnp.transpose(integrals, (1, 0, 2)),
        firsts.reshape(1, LANES),
        slab_irrep.astype(jnp.float32).reshape(1, slab),
        after,
    )


def spread_kernel(
    folds, second_width, rest, parts, here_ref, amp_ref, out_ref,
    wide, strided, shifted, stage,
):
    virt = amp_ref.shape[1]
    tiles = wide.shape[0]
    tall = virt // folds
    last = (tiles - 1) * LANES
    early = iota((tall, LANES), 1) < LANES // 2
    for t in range(tiles):
        if t < tiles - 1:
            wide[t] = amp_ref[0, :, t * LANES : (t + 1) * LANES].astype(jnp.float32)
        else:
            wide[t] = jnp.zeros((virt, LANES), jnp.float32)
            wide[t, :, : virt - last] = amp_ref[0, :, last:].astype(jnp.float32)
    for f in range(folds):
        held = None
        for t in range(tiles):
            piece = wide[t, pl.ds(f, tall, stride=folds), :]
            strided[f, :, t * LANES : (t + 1) * LANES] = piece.astype(jnp.bfloat16)
            rolled = pltpu.roll(piece, LANES // 2, 1)
            if t > 0:
                shifted[f, :, (t - 1) * LANES : t * LANES] = jnp.where(
                    early, held, rolled
                ).astype(jnp.bfloat16)
            held = rolled
    span = 2 * second_width
    source = iota((LANES, 1), 0)
    lane = iota((LANES, 2 * LANES), 1)
    slots = rest // parts // 2
    for w in range(rest // 2):
        tile, offset = divmod(span * w, LANES)
        held = strided
        if offset + span > LANES:
            held, offset = shifted, offset - LANES // 2
        column = source - offset
        inside = (column >= 0) & (column < span)
        target = column + jnp.where(column >= second_width, LANES - second_width, 0)
        target = jnp.where(inside, target, -LANES)
        at = slice(tile * LANES, (tile + 1) * LANES)
        select = jnp.concatenate(
            [one_hot(lane == target + f * second_width) for f in range(folds)], axis=0
        )
        total = dot(jnp.concatenate([held[f, :, at] for f in range(folds)], axis=1), select)
        for a in range(2):
            outer, inner = divmod(2 * w + a, parts)
            away = lax.rem(outer - here_ref[0] + rest // parts, rest // parts)
            place = sum(jnp.where(away == k, AWAYS.index(k), 0) for k in AWAYS)
            half = place // slots
            stage[half, inner, pl.ds(place - half * slots, tall, stride=slots), :] = total[
                :, a * LANES : (a + 1) * LANES
            ]
    owners = out_ref.shape[1]
    rows = out_ref.shape[3] // 2
    for inner in range(parts):
        for i in range(owners):
            for half in range(2):
                out_ref[inner, i, 0, half * rows : (half + 1) * rows] = stage[
                    half, inner, i * rows : (i + 1) * rows, :
                ].astype(jnp.bfloat16)


def spread_amplitudes(here, amplitudes, owners, outer, parts):
    pairs, virt, _ = amplitudes.shape
    rest = outer * parts
    second_width = virt // rest
    folds = LANES // second_width
    tiles = -(-virt // LANES)
    tall = virt // folds
    rows = tall // owners * outer
    return pl.pallas_call(
        functools.partial(spread_kernel, folds, second_width, rest, parts),
        grid=(pairs,),
        in_specs=[
            pl.BlockSpec(memory_space=pltpu.SMEM),
            pl.BlockSpec((1, virt, virt), lambda p: (p, 0, 0)),
        ],
        out_specs=pl.BlockSpec((parts, owners, 1, rows, LANES), lambda p: (0, 0, p, 0, 0)),
        out_shape=jax.ShapeDtypeStruct((parts, owners, pairs, rows, LANES), jnp.bfloat16),
        scratch_shapes=[
            pltpu.VMEM((tiles, virt, LANES), jnp.float32),
            pltpu.VMEM((folds, tall, tiles * LANES), jnp.bfloat16),
            pltpu.VMEM((folds, tall, (tiles - 1) * LANES), jnp.bfloat16),
            pltpu.VMEM((2, parts, tall * outer // 2, LANES), jnp.float32),
        ],
        compiler_params=pltpu.CompilerParams(
            dimension_semantics=("arbitrary",), vmem_limit_bytes=56 * MIB
        ),
        cost_estimate=pl.CostEstimate(
            flops=2 * 480 * 80 * 65536, bytes_accessed=8_000_000, transcendentals=0
        ),
        name="spread_amplitudes",
    )(here, amplitudes)


def masked_rows(left, at, piece, label):
    tall = piece.shape[0]
    for g in range(IRREPS):
        left[g * tall : (g + 1) * tall, at : at + LANES] = piece * one_hot(label == g)


def contract_kernel(tile, slots, shards, half, amp_ref, labels_ref, *refs):
    refs = list(refs)
    first = half == 0
    start_ref = None if first else refs.pop(0)
    blocks = [(refs[2 * k], refs[2 * k + 1]) for k in range(shards)]
    refs = refs[2 * shards :]
    out_ref = refs.pop(0)
    rest_ref = refs.pop(0) if shards < slots else None
    (amps, labels, turned, left_a, left_b, right, spares, swap,
     amp_sems, block_sems, spare_sems, one_sems) = refs
    all_pairs = amps.shape[1]
    steps = amps.shape[0]
    groups = right.shape[0]
    per_quarter = groups // QUARTERS
    each = tile // slots
    square = tile * tile
    chunk = 2 * all_pairs

    def amp_copy(k):
        at = pl.ds(half * steps * tile + k * tile, tile)
        return pltpu.make_async_copy(amp_ref.at[:, at], amps.at[k], amp_sems.at[k])

    copies = []
    split, cut = groups // 2, per_quarter // 2
    for k, pair in enumerate(blocks):
        for h, block in enumerate(pair):
            copies.append(
                pltpu.make_async_copy(
                    block.at[pl.ds(0, split)],
                    right.at[pl.ds(h * split, split), k, :, pl.ds(0, LANES)],
                    block_sems.at[2 * k + h],
                )
            )
            count = (cut, per_quarter - cut)[h]
            copies.append(
                pltpu.make_async_copy(
                    block.at[pl.ds(split, count)],
                    spares.at[k, pl.ds(h * cut, count)],
                    spare_sems.at[2 * k + h],
                )
            )
    if not first:
        copies.append(pltpu.make_async_copy(start_ref, out_ref, one_sems.at[0]))
    labels_copy = pltpu.make_async_copy(labels_ref, labels, one_sems.at[1])
    amp_copies = [amp_copy(k) for k in range(steps)]
    amp_copies[0].start()
    labels_copy.start()
    for copy in copies:
        copy.start()
    for copy in amp_copies[1:]:
        copy.start()
    order = iota((square, square), 0)
    swap[...] = one_hot(iota((square, square), 1) == (order % tile) * tile + order // tile)
    quarter = iota((1, LANES), 1) // SPARE
    labels_copy.wait()

    def build(k, left):
        amp_copies[k].wait()
        for p in range(0, all_pairs, 2 * tile):
            pieces = [amps[k, q : q + tile].reshape(square, LANES) for q in (p, p + tile)]
            done = dot(swap[...], jnp.concatenate(pieces, axis=1)).astype(jnp.bfloat16)
            for r in range(tile):
                for h in range(2):
                    turned[k % 2, r, p + h * tile : p + (h + 1) * tile, :] = done[
                        r * tile : (r + 1) * tile, h * LANES : (h + 1) * LANES
                    ]
        for r in range(tile):
            group, slot = divmod(r, slots)
            if slot < shards:
                label = labels[k * tile + r : k * tile + r + 1, :]
                masked_rows(left, (group * shards + slot) * LANES, turned[k % 2, r], label)
            else:
                rest_ref[k * each + group] = turned[k % 2, r]

    lefts = (left_a, left_b)
    build(0, left_a)
    for copy in copies:
        copy.wait()
    for c in range(groups):
        keep = one_hot(quarter == c // per_quarter)
        for k in range(shards):
            right[c, k, :, LANES:] = spares[k, c % per_quarter] * keep
    for k in range(steps):
        if k + 1 < steps:
            build(k + 1, lefts[(k + 1) % 2])
        block = right[k * each : (k + 1) * each].reshape(each * shards * LANES, 2 * LANES)
        left = lefts[k % 2]
        for m in range(0, left.shape[0], chunk):
            product = dot(left[m : m + chunk], block)
            if first and k == 0:
                out_ref[m : m + chunk] = product
            else:
                out_ref[m : m + chunk] += product


def contract(amplitudes, labels, start, blocks, half):
    all_pairs, rows, _ = amplitudes.shape
    tile = 16
    slots = 4
    shards = len(blocks)
    groups = rows // (2 * slots)
    per_quarter = groups // QUARTERS
    whole = pl.BlockSpec(memory_space=pltpu.VMEM)
    hbm = pl.BlockSpec(memory_space=pl.ANY)
    steps = rows // 2 // tile
    tall = IRREPS * all_pairs
    wide = tile // slots * shards * LANES
    operands = (() if half == 0 else (start,)) + tuple(sum(blocks, ()))
    out_shape = [jax.ShapeDtypeStruct((tall, 2 * LANES), jnp.float32)]
    if shards < slots:
        out_shape.append(jax.ShapeDtypeStruct((groups, all_pairs, LANES), jnp.bfloat16))
    return pl.pallas_call(
        functools.partial(contract_kernel, tile, slots, shards, half),
        in_specs=[hbm] * (2 + len(operands)),
        out_specs=[whole] * len(out_shape),
        out_shape=out_shape,
        scratch_shapes=[
            pltpu.VMEM((steps, all_pairs, tile, LANES), jnp.bfloat16),
            pltpu.VMEM(labels.shape, labels.dtype),
            pltpu.VMEM((2, tile, all_pairs, LANES), jnp.bfloat16),
            pltpu.VMEM((tall, wide), jnp.bfloat16),
            pltpu.VMEM((tall, wide), jnp.bfloat16),
            pltpu.VMEM((groups, shards, LANES, 2 * LANES), jnp.bfloat16),
            pltpu.VMEM((shards, per_quarter, LANES, LANES), jnp.bfloat16),
            pltpu.VMEM((tile * tile, tile * tile), jnp.bfloat16),
            pltpu.SemaphoreType.DMA((steps,)),
            pltpu.SemaphoreType.DMA((2 * shards,)),
            pltpu.SemaphoreType.DMA((2 * shards,)),
            pltpu.SemaphoreType.DMA((2,)),
        ],
        compiler_params=pltpu.CompilerParams(vmem_limit_bytes=(26 if half else 56) * MIB),
        cost_estimate=pl.CostEstimate(
            flops=2 * 768 * 10240 * 256, bytes_accessed=6_000_000, transcendentals=0
        ),
        name="contract",
    )(amplitudes, labels, *operands)


def last_kernel(pairs, slots, cores, core_ref, rest_hbm, labels_hbm, start_hbm, low_hbm, high_hbm,
                mine_ref, other_ref, rest, labels, start, left, right, spares, main, over, sems):
    groups, all_pairs, _ = rest.shape
    per_quarter = groups // QUARTERS
    split, cut = groups // 2, per_quarter // 2
    half = pl.ds(0, LANES)
    first = [
        pltpu.make_async_copy(rest_hbm, rest, sems.at[0]),
        pltpu.make_async_copy(labels_hbm, labels, sems.at[1]),
    ]
    second = [
        pltpu.make_async_copy(
            low_hbm.at[pl.ds(0, split)], right.at[pl.ds(0, split), :, half], sems.at[2]
        ),
        pltpu.make_async_copy(
            high_hbm.at[pl.ds(0, split)], right.at[pl.ds(split, split), :, half], sems.at[3]
        ),
        pltpu.make_async_copy(low_hbm.at[pl.ds(split, cut)], spares.at[pl.ds(0, cut)], sems.at[4]),
        pltpu.make_async_copy(
            high_hbm.at[pl.ds(split, per_quarter - cut)],
            spares.at[pl.ds(cut, per_quarter - cut)],
            sems.at[5],
        ),
    ]
    third = pltpu.make_async_copy(start_hbm, start, sems.at[6])
    for copy in first + second + [third]:
        copy.start()
    for copy in first:
        copy.wait()
    quarter = iota((1, LANES), 1) // SPARE
    for c in range(groups):
        row = c * slots + slots - 1
        masked_rows(left, c * LANES, rest[c], labels[row : row + 1, :])
    for copy in second:
        copy.wait()
    for c in range(groups):
        right[c, :, LANES:] = spares[c % per_quarter] * one_hot(quarter == c // per_quarter)
    product = dot(left[...], right[...].reshape(groups * LANES, 2 * LANES))
    third.wait()
    total = start[...] + product
    main[...] = total[:, :LANES]
    spare = total[:, LANES:]
    spare = spare + pltpu.roll(spare, 2 * SPARE, 1)
    over[...] = spare + pltpu.roll(spare, SPARE, 1)
    owners = all_pairs // pairs
    lines = mine_ref.shape[0] // (owners // cores)
    run = 8
    per = IRREPS // QUARTERS

    def emit(core, ref):
        ref[...] = jnp.zeros_like(ref)
        for block in range(owners // cores // run):
            owner = (block * cores + core) * run
            base = block * run * lines
            for g in range(IRREPS):
                for p in range(pairs):
                    at = g * all_pairs + owner * pairs + p
                    ref[pl.ds(base + g * pairs + p, run, stride=lines), :] = main[
                        pl.ds(at, run, stride=pairs), :
                    ]
            for g in range(per):
                for p in range(pairs):
                    value = jnp.zeros((run, LANES), jnp.float32)
                    for q in range(QUARTERS):
                        at = (q * per + g) * all_pairs + owner * pairs + p
                        piece = over[pl.ds(at, run, stride=pairs), :]
                        value = value + jnp.where(quarter == q, piece, 0.0)
                    at = base + (IRREPS + g) * pairs + p
                    ref[pl.ds(at, run, stride=lines), :] = value

    for core in range(cores):

        @pl.when(core_ref[0] == core)
        def _():
            emit(core, mine_ref)

        @pl.when(core_ref[0] != core)
        def _():
            emit(core, other_ref)


def contract_last(core, rest, labels, start, low, high, pairs):
    groups, all_pairs, _ = rest.shape
    cores = 2
    owners = all_pairs // pairs
    lines = -(-(IRREPS + IRREPS // QUARTERS) * pairs // 8) * 8
    whole = pl.BlockSpec(memory_space=pltpu.VMEM)
    hbm = pl.BlockSpec(memory_space=pl.ANY)
    tall = IRREPS * all_pairs
    shape = jax.ShapeDtypeStruct((owners // cores * lines, LANES), jnp.float32)
    return pl.pallas_call(
        functools.partial(last_kernel, pairs, labels.shape[0] // groups, cores),
        in_specs=[pl.BlockSpec(memory_space=pltpu.SMEM)] + [hbm] * 5,
        out_specs=[whole, whole],
        out_shape=[shape, shape],
        scratch_shapes=[
            pltpu.VMEM(rest.shape, rest.dtype),
            pltpu.VMEM(labels.shape, labels.dtype),
            pltpu.VMEM(start.shape, start.dtype),
            pltpu.VMEM((tall, groups * LANES), jnp.bfloat16),
            pltpu.VMEM((groups, LANES, 2 * LANES), jnp.bfloat16),
            pltpu.VMEM((groups // QUARTERS, LANES, LANES), jnp.bfloat16),
            pltpu.VMEM((tall, LANES), jnp.float32),
            pltpu.VMEM((tall, LANES), jnp.float32),
            pltpu.SemaphoreType.DMA((7,)),
        ],
        compiler_params=pltpu.CompilerParams(vmem_limit_bytes=18 * MIB),
        cost_estimate=pl.CostEstimate(
            flops=2 * 768 * 2560 * 256, bytes_accessed=3_000_000, transcendentals=0
        ),
        name="contract_last",
    )(core, rest, labels, start, low, high)


def unpack_kernel(pairs, round_ref, parts_ref, rank_ref, slab_ref, rest_ref, out_ref):
    rows = parts_ref.shape[1]
    slab = slab_ref.shape[1]
    summed = parts_ref[0]
    for k in range(1, parts_ref.shape[0]):
        summed = summed + parts_ref[k]
    irrep = slab_ref[...]
    rank = rank_ref[...] - round_ref[0] * CAP
    each = IRREPS // QUARTERS
    inside = (rank >= 0) & (rank < CAP)
    spare = rank >= LANES
    target = jnp.where(spare, (irrep // each) * SPARE + rank - LANES, rank)
    target = jnp.where(inside, target, -1)
    pick = jnp.where(iota((LANES, slab), 0) == target, 1.0, 0.0)
    values = jnp.dot(
        summed, pick, preferred_element_type=jnp.float32, precision=lax.Precision.HIGHEST
    )
    first = jnp.where(spare, (IRREPS + irrep % each) * pairs, irrep * pairs)
    row = iota((rows, slab), 0)
    for p in range(pairs):
        out_ref[p : p + 1, :] = rest_ref[p : p + 1, :] + jnp.sum(
            jnp.where(row == first + p, values, 0.0), axis=0, keepdims=True
        )


def unpack(which, parts, rank, slab_irrep, rest):
    pairs, slab = rest.shape
    whole = pl.BlockSpec(memory_space=pltpu.VMEM)
    return pl.pallas_call(
        functools.partial(unpack_kernel, pairs),
        in_specs=[pl.BlockSpec(memory_space=pltpu.SMEM), whole, whole, whole, whole],
        out_specs=whole,
        out_shape=jax.ShapeDtypeStruct((pairs, slab), jnp.float32),
        compiler_params=pltpu.CompilerParams(vmem_limit_bytes=6 * MIB),
        name="unpack",
    )(which, parts, rank, slab_irrep.reshape(1, slab), rest)


def local(amplitudes, integrals, virt_irrep, slab_irrep):
    pairs = amplitudes.shape[0]
    owners = lax.axis_size("va")
    count = lax.axis_size("vb")
    parts = lax.axis_size("occ")
    first_width, second_width, _ = integrals.shape
    folds = LANES // second_width
    groups = first_width // folds
    here = lax.axis_index("vb")
    part = lax.axis_index("occ")

    first_labels = lax.dynamic_slice_in_dim(
        virt_irrep, lax.axis_index("va") * first_width, first_width, 0
    )
    second_labels = lax.dynamic_index_in_dim(
        virt_irrep.reshape(count, parts, second_width), part, 1, keepdims=False
    )
    own_labels = lax.dynamic_index_in_dim(second_labels, here, 0, keepdims=False)
    order = lax.rem(here + jnp.array(AWAYS, jnp.int32), count)
    labels = jnp.bitwise_xor(
        first_labels.reshape(groups, 1, folds, 1),
        jnp.take(second_labels, order, axis=0).reshape(1, count, 1, second_width),
    ).reshape(groups, count, folds * second_width)
    labels = jnp.pad(
        labels, ((0, 0), (0, 0), (0, LANES - folds * second_width)), constant_values=-1
    )
    near_labels = labels[:, : count // 2].reshape(-1, LANES)
    far_labels = labels[:, count // 2 :].reshape(-1, LANES)

    up = [(i, (i + 1) % count) for i in range(count)]
    down = [(i, (i - 1) % count) for i in range(count)]

    same_core = [
        [(2 * k + core) * owners + i for k in range(parts // 2) for i in range(owners)]
        for core in range(2)
    ]

    def shifted(pair, perm):
        return tuple(lax.ppermute(block, "vb", perm) for block in pair)

    def blocks_of(which, after):
        low, high, rank = pack_integrals(
            which, integrals, first_labels, own_labels, slab_irrep, after
        )
        packed = low, high
        r1, l1 = shifted(packed, up), shifted(packed, down)
        r2, l2 = shifted(r1, up), shifted(l1, down)
        r3, l3 = shifted(r2, up), shifted(l2, down)
        return (packed, l1, r1, l2), (r2, r3, l3), rank

    def finish(which, near, middle, rank, arrived, rest_of_sum):
        (start,) = contract(arrived, near_labels, None, near, 0)
        up_end, down_end, start = lax.optimization_barrier((middle[1][0], middle[2][1], start))
        far = lax.ppermute(up_end, "vb", up), lax.ppermute(down_end, "vb", down)
        start, rest_of_sum = lax.optimization_barrier((start, rest_of_sum))
        start, rest = contract(arrived, far_labels, start, middle, 1)
        core = lax.rem(part, 2)
        mine, other = contract_last(core.reshape(1), rest, far_labels, start, *far, pairs)
        partial = mine + lax.ppermute(other, "occ", [(i, i ^ 1) for i in range(parts)])
        partial = partial.reshape(parts // 2 * owners, -1, LANES)
        summands = lax.all_to_all(
            partial, SOURCES, split_axis=0, concat_axis=0, tiled=True, axis_index_groups=same_core
        )
        return unpack(which, summands, rank, slab_irrep, rest_of_sum)

    first = jnp.zeros((1,), jnp.int32)
    spread = spread_amplitudes(here.reshape(1), amplitudes, owners, count, parts)
    sent = spread.reshape((parts * owners,) + spread.shape[2:])
    arrived = lax.all_to_all(sent, SOURCES, split_axis=0, concat_axis=0, tiled=True)
    arrived = arrived.reshape((parts * owners * pairs,) + spread.shape[3:])
    near, middle, rank = blocks_of(first, spread)
    largest = jnp.max(rank)

    def more(carry):
        return carry[0] * CAP <= largest

    def step(carry):
        which = carry[0].reshape(1)
        near, middle, rank = blocks_of(which, spread)
        return carry[0] + 1, finish(which, near, middle, rank, arrived, carry[1])

    nothing = jnp.zeros((pairs, slab_irrep.shape[0]), jnp.float32)
    later = lax.while_loop(more, step, (jnp.int32(1), nothing))[1]
    return finish(first, near, middle, rank, arrived, later)


def solution(mesh):
    return jax.shard_map(
        local,
        mesh=mesh,
        in_specs=(P(("va", "vb", "occ"), None, None), P("va", ("vb", "occ"), None), P(), P()),
        out_specs=P(("va", "vb", "occ"), None),
        check_vma=False,
    )
```

```python
import functools

import jax
import jax.numpy as jnp
from jax import lax
from jax.experimental import pallas as pl
from jax.experimental.pallas import tpu as pltpu
from jax.sharding import PartitionSpec as P

LANES = 128
IRREPS = 8
SPARE = 32
CAP = LANES + SPARE
QUARTERS = LANES // SPARE
MIB = 1024 * 1024
SOURCES = ("occ", "va")
AWAYS = (0, 1, 7, 2, 6, 5, 3, 4)


def iota(shape, axis):
    return lax.broadcasted_iota(jnp.int32, shape, axis)


def one_hot(hits):
    return jnp.where(hits, 1.0, 0.0).astype(jnp.bfloat16)


def dot(a, b):
    return jnp.dot(a, b, preferred_element_type=jnp.float32)


def pack_kernel(
    folds, round_ref, second_ref, block_ref, first_ref, row_ref, after_ref,
    low_ref, high_ref, rank_ref, onehot, firsts, masked, part_main, part_over, main, over,
):
    del after_ref
    step = pl.program_id(0)
    per_step, first_width, slab = block_ref.shape
    second_width = per_step * pl.num_programs(0)
    pitch = masked.shape[0] // per_step
    groups = first_width // folds
    square = (LANES, LANES)

    def turned(vector):
        return jnp.transpose(jnp.broadcast_to(vector, square))

    @pl.when(step == 0)
    def _():
        masked[...] = jnp.zeros_like(masked)
        for pad in range(folds * second_width, LANES):
            rows = pl.ds(pad, groups, stride=LANES)
            main[rows, :] = jnp.zeros((groups, LANES), jnp.float32)
            over[rows, :] = jnp.zeros((groups, LANES), jnp.float32)
        firsts[...] = turned(first_ref[...])[: firsts.shape[0]]
        offset = (round_ref[0] * CAP).astype(jnp.float32)
        before = one_hot(iota(square, 0) < iota(square, 1))
        lane = iota((LANES, 2 * LANES), 1).astype(jnp.float32)
        base = jnp.zeros((IRREPS, 1), jnp.float32)
        for k in range(slab // LANES):
            at = slice(k * LANES, (k + 1) * LANES)
            own = iota((IRREPS, LANES), 0).astype(jnp.float32) == row_ref[:, at]
            member = jnp.where(own, 1.0, 0.0)
            count = dot(member.astype(jnp.bfloat16), before) + base
            rank = jnp.sum(jnp.where(own, count, 0.0), axis=0, keepdims=True)
            rank_ref[:, at] = rank.astype(jnp.int32)
            base = base + jnp.sum(member, axis=1, keepdims=True)
            column = turned(rank) - offset
            onehot[at, :] = one_hot(lane == jnp.concatenate([column, column], axis=1))

    for k in range(per_step):
        second = second_ref[step * per_step + k]
        wanted = jnp.bitwise_xor(firsts[...].astype(jnp.int32), second).astype(jnp.float32)
        wanted = wanted[:first_width]
        for t in range(slab // LANES):
            at = slice(t * LANES, (t + 1) * LANES)
            allowed = wanted == row_ref[:, at]
            values = jnp.where(allowed, block_ref[k, :, at].astype(jnp.float32), 0.0)
            masked[k * pitch : k * pitch + first_width, at] = values.astype(jnp.bfloat16)
    packed = dot(masked[...], onehot[...])
    part_main[...] = packed[:, :LANES]
    part_over[...] = packed[:, LANES:]
    for k in range(per_step):
        d = step * per_step + k
        for f in range(folds):
            source = pl.ds(k * pitch + f, groups, stride=folds)
            target = pl.ds(f * second_width + d, groups, stride=LANES)
            main[target, :] = part_main[source, :]
            over[target, :] = part_over[source, :]

    @pl.when(step == pl.num_programs(0) - 1)
    def _():
        per_quarter = groups // QUARTERS
        low = iota(square, 1) < SPARE
        split = groups // 2
        for e in range(per_quarter):
            spare = jnp.zeros(square, jnp.float32)
            for q in range(QUARTERS):
                group = q * per_quarter + e
                rows = slice(group * LANES, (group + 1) * LANES)
                packed = main[rows, :].astype(jnp.bfloat16)
                if group < split:
                    low_ref[group] = packed
                else:
                    high_ref[group - split] = packed
                piece = jnp.where(low, over[rows, :], 0.0)
                spare = spare + (piece if q == 0 else pltpu.roll(piece, q * SPARE, 1))
            spare = spare.astype(jnp.bfloat16)
            if e < per_quarter // 2:
                low_ref[split + e] = spare
            else:
                high_ref[split + e - per_quarter // 2] = spare


def pack_integrals(which, integrals, first_labels, second_labels, slab_irrep, after):
    first_width, second_width, slab = integrals.shape
    folds = LANES // second_width
    groups = first_width // folds
    per_step = 5
    pitch = -(-first_width // 16) * 16
    low = groups // 2 + groups // QUARTERS // 2
    high = groups + groups // QUARTERS - low
    smem = pl.BlockSpec(memory_space=pltpu.SMEM)
    whole = pl.BlockSpec(memory_space=pltpu.VMEM)
    firsts = jnp.pad(first_labels, (0, LANES - first_width)).astype(jnp.float32)
    return pl.pallas_call(
        functools.partial(pack_kernel, folds),
        grid=(second_width // per_step,),
        in_specs=[
            smem,
            smem,
            pl.BlockSpec((per_step, first_width, slab), lambda i: (i, 0, 0)),
            whole,
            whole,
            pl.BlockSpec(memory_space=pl.ANY),
        ],
        out_specs=[whole, whole, whole],
        out_shape=[
            jax.ShapeDtypeStruct((low, LANES, LANES), jnp.bfloat16),
            jax.ShapeDtypeStruct((high, LANES, LANES), jnp.bfloat16),
            jax.ShapeDtypeStruct((1, slab), jnp.int32),
        ],
        scratch_shapes=[
            pltpu.VMEM((slab, 2 * LANES), jnp.bfloat16),
            pltpu.VMEM((pitch, LANES), jnp.float32),
            pltpu.VMEM((per_step * pitch, slab), jnp.bfloat16),
            pltpu.VMEM((per_step * pitch, LANES), jnp.float32),
            pltpu.VMEM((per_step * pitch, LANES), jnp.float32),
            pltpu.VMEM((groups * LANES, LANES), jnp.float32),
            pltpu.VMEM((groups * LANES, LANES), jnp.float32),
        ],
        compiler_params=pltpu.CompilerParams(
            dimension_semantics=("arbitrary",), vmem_limit_bytes=16 * MIB
        ),
        cost_estimate=pl.CostEstimate(
            flops=2 * 2600 * slab * 256, bytes_accessed=6_000_000, transcendentals=0
        ),
        name="pack_integrals",
    )(
        which,
        second_labels,
        jnp.transpose(integrals, (1, 0, 2)),
        firsts.reshape(1, LANES),
        slab_irrep.astype(jnp.float32).reshape(1, slab),
        after,
    )


def spread_kernel(
    folds, second_width, rest, parts, here_ref, amp_ref, out_ref,
    wide, strided, shifted, stage,
):
    virt = amp_ref.shape[1]
    tiles = wide.shape[0]
    tall = virt // folds
    last = (tiles - 1) * LANES
    early = iota((tall, LANES), 1) < LANES // 2
    for t in range(tiles):
        if t < tiles - 1:
            wide[t] = amp_ref[0, :, t * LANES : (t + 1) * LANES].astype(jnp.float32)
        else:
            wide[t] = jnp.zeros((virt, LANES), jnp.float32)
            wide[t, :, : virt - last] = amp_ref[0, :, last:].astype(jnp.float32)
    for f in range(folds):
        held = None
        for t in range(tiles):
            piece = wide[t, pl.ds(f, tall, stride=folds), :]
            strided[f, :, t * LANES : (t + 1) * LANES] = piece.astype(jnp.bfloat16)
            rolled = pltpu.roll(piece, LANES // 2, 1)
            if t > 0:
                shifted[f, :, (t - 1) * LANES : t * LANES] = jnp.where(
                    early, held, rolled
                ).astype(jnp.bfloat16)
            held = rolled
    span = 2 * second_width
    source = iota((LANES, 1), 0)
    lane = iota((LANES, 2 * LANES), 1)
    slots = rest // parts // 2
    for w in range(rest // 2):
        tile, offset = divmod(span * w, LANES)
        held = strided
        if offset + span > LANES:
            held, offset = shifted, offset - LANES // 2
        column = source - offset
        inside = (column >= 0) & (column < span)
        target = column + jnp.where(column >= second_width, LANES - second_width, 0)
        target = jnp.where(inside, target, -LANES)
        at = slice(tile * LANES, (tile + 1) * LANES)
        select = jnp.concatenate(
            [one_hot(lane == target + f * second_width) for f in range(folds)], axis=0
        )
        total = dot(jnp.concatenate([held[f, :, at] for f in range(folds)], axis=1), select)
        for a in range(2):
            outer, inner = divmod(2 * w + a, parts)
            away = lax.rem(outer - here_ref[0] + rest // parts, rest // parts)
            place = sum(jnp.where(away == k, AWAYS.index(k), 0) for k in AWAYS)
            half = place // slots
            stage[half, inner, pl.ds(place - half * slots, tall, stride=slots), :] = total[
                :, a * LANES : (a + 1) * LANES
            ]
    owners = out_ref.shape[1]
    rows = out_ref.shape[3] // 2
    for inner in range(parts):
        for i in range(owners):
            for half in range(2):
                out_ref[inner, i, 0, half * rows : (half + 1) * rows] = stage[
                    half, inner, i * rows : (i + 1) * rows, :
                ].astype(jnp.bfloat16)


def spread_amplitudes(here, amplitudes, owners, outer, parts):
    pairs, virt, _ = amplitudes.shape
    rest = outer * parts
    second_width = virt // rest
    folds = LANES // second_width
    tiles = -(-virt // LANES)
    tall = virt // folds
    rows = tall // owners * outer
    return pl.pallas_call(
        functools.partial(spread_kernel, folds, second_width, rest, parts),
        grid=(pairs,),
        in_specs=[
            pl.BlockSpec(memory_space=pltpu.SMEM),
            pl.BlockSpec((1, virt, virt), lambda p: (p, 0, 0)),
        ],
        out_specs=pl.BlockSpec((parts, owners, 1, rows, LANES), lambda p: (0, 0, p, 0, 0)),
        out_shape=jax.ShapeDtypeStruct((parts, owners, pairs, rows, LANES), jnp.bfloat16),
        scratch_shapes=[
            pltpu.VMEM((tiles, virt, LANES), jnp.float32),
            pltpu.VMEM((folds, tall, tiles * LANES), jnp.bfloat16),
            pltpu.VMEM((folds, tall, (tiles - 1) * LANES), jnp.bfloat16),
            pltpu.VMEM((2, parts, tall * outer // 2, LANES), jnp.float32),
        ],
        compiler_params=pltpu.CompilerParams(
            dimension_semantics=("arbitrary",), vmem_limit_bytes=56 * MIB
        ),
        cost_estimate=pl.CostEstimate(
            flops=2 * 480 * 80 * 65536, bytes_accessed=8_000_000, transcendentals=0
        ),
        name="spread_amplitudes",
    )(here, amplitudes)


def masked_rows(left, at, piece, label):
    tall = piece.shape[0]
    for g in range(IRREPS):
        left[g * tall : (g + 1) * tall, at : at + LANES] = piece * one_hot(label == g)


def contract_kernel(tile, slots, shards, half, amp_ref, labels_ref, *refs):
    refs = list(refs)
    first = half == 0
    start_ref = None if first else refs.pop(0)
    blocks = [(refs[2 * k], refs[2 * k + 1]) for k in range(shards)]
    refs = refs[2 * shards :]
    out_ref = refs.pop(0)
    rest_ref = refs.pop(0) if shards < slots else None
    (amps, labels, turned, left_a, left_b, right, spares, swap,
     amp_sems, block_sems, spare_sems, one_sems) = refs
    all_pairs = amps.shape[1]
    steps = amps.shape[0]
    groups = right.shape[0]
    per_quarter = groups // QUARTERS
    each = tile // slots
    square = tile * tile
    chunk = 2 * all_pairs

    def amp_copy(k):
        at = pl.ds(half * steps * tile + k * tile, tile)
        return pltpu.make_async_copy(amp_ref.at[:, at], amps.at[k], amp_sems.at[k])

    copies = []
    split, cut = groups // 2, per_quarter // 2
    for k, pair in enumerate(blocks):
        for h, block in enumerate(pair):
            copies.append(
                pltpu.make_async_copy(
                    block.at[pl.ds(0, split)],
                    right.at[pl.ds(h * split, split), k, :, pl.ds(0, LANES)],
                    block_sems.at[2 * k + h],
                )
            )
            count = (cut, per_quarter - cut)[h]
            copies.append(
                pltpu.make_async_copy(
                    block.at[pl.ds(split, count)],
                    spares.at[k, pl.ds(h * cut, count)],
                    spare_sems.at[2 * k + h],
                )
            )
    if not first:
        copies.append(pltpu.make_async_copy(start_ref, out_ref, one_sems.at[0]))
    labels_copy = pltpu.make_async_copy(labels_ref, labels, one_sems.at[1])
    amp_copies = [amp_copy(k) for k in range(steps)]
    amp_copies[0].start()
    labels_copy.start()
    for copy in copies:
        copy.start()
    for copy in amp_copies[1:]:
        copy.start()
    order = iota((square, square), 0)
    swap[...] = one_hot(iota((square, square), 1) == (order % tile) * tile + order // tile)
    quarter = iota((1, LANES), 1) // SPARE
    labels_copy.wait()

    def build(k, left):
        amp_copies[k].wait()
        for p in range(0, all_pairs, 2 * tile):
            pieces = [amps[k, q : q + tile].reshape(square, LANES) for q in (p, p + tile)]
            done = dot(swap[...], jnp.concatenate(pieces, axis=1)).astype(jnp.bfloat16)
            for r in range(tile):
                for h in range(2):
                    turned[k % 2, r, p + h * tile : p + (h + 1) * tile, :] = done[
                        r * tile : (r + 1) * tile, h * LANES : (h + 1) * LANES
                    ]
        for r in range(tile):
            group, slot = divmod(r, slots)
            if slot < shards:
                label = labels[k * tile + r : k * tile + r + 1, :]
                masked_rows(left, (group * shards + slot) * LANES, turned[k % 2, r], label)
            else:
                rest_ref[k * each + group] = turned[k % 2, r]

    lefts = (left_a, left_b)
    build(0, left_a)
    for copy in copies:
        copy.wait()
    for c in range(groups):
        keep = one_hot(quarter == c // per_quarter)
        for k in range(shards):
            right[c, k, :, LANES:] = spares[k, c % per_quarter] * keep
    for k in range(steps):
        if k + 1 < steps:
            build(k + 1, lefts[(k + 1) % 2])
        block = right[k * each : (k + 1) * each].reshape(each * shards * LANES, 2 * LANES)
        left = lefts[k % 2]
        for m in range(0, left.shape[0], chunk):
            product = dot(left[m : m + chunk], block)
            if first and k == 0:
                out_ref[m : m + chunk] = product
            else:
                out_ref[m : m + chunk] += product


def contract(amplitudes, labels, start, blocks, half):
    all_pairs, rows, _ = amplitudes.shape
    tile = 16
    slots = 4
    shards = len(blocks)
    groups = rows // (2 * slots)
    per_quarter = groups // QUARTERS
    whole = pl.BlockSpec(memory_space=pltpu.VMEM)
    hbm = pl.BlockSpec(memory_space=pl.ANY)
    steps = rows // 2 // tile
    tall = IRREPS * all_pairs
    wide = tile // slots * shards * LANES
    operands = (() if half == 0 else (start,)) + tuple(sum(blocks, ()))
    out_shape = [jax.ShapeDtypeStruct((tall, 2 * LANES), jnp.float32)]
    if shards < slots:
        out_shape.append(jax.ShapeDtypeStruct((groups, all_pairs, LANES), jnp.bfloat16))
    return pl.pallas_call(
        functools.partial(contract_kernel, tile, slots, shards, half),
        in_specs=[hbm] * (2 + len(operands)),
        out_specs=[whole] * len(out_shape),
        out_shape=out_shape,
        scratch_shapes=[
            pltpu.VMEM((steps, all_pairs, tile, LANES), jnp.bfloat16),
            pltpu.VMEM(labels.shape, labels.dtype),
            pltpu.VMEM((2, tile, all_pairs, LANES), jnp.bfloat16),
            pltpu.VMEM((tall, wide), jnp.bfloat16),
            pltpu.VMEM((tall, wide), jnp.bfloat16),
            pltpu.VMEM((groups, shards, LANES, 2 * LANES), jnp.bfloat16),
            pltpu.VMEM((shards, per_quarter, LANES, LANES), jnp.bfloat16),
            pltpu.VMEM((tile * tile, tile * tile), jnp.bfloat16),
            pltpu.SemaphoreType.DMA((steps,)),
            pltpu.SemaphoreType.DMA((2 * shards,)),
            pltpu.SemaphoreType.DMA((2 * shards,)),
            pltpu.SemaphoreType.DMA((2,)),
        ],
        compiler_params=pltpu.CompilerParams(vmem_limit_bytes=(26 if half else 56) * MIB),
        cost_estimate=pl.CostEstimate(
            flops=2 * 768 * 10240 * 256, bytes_accessed=6_000_000, transcendentals=0
        ),
        name="contract",
    )(amplitudes, labels, *operands)


def last_kernel(pairs, slots, cores, core_ref, rest_hbm, labels_hbm, start_hbm, low_hbm, high_hbm,
                mine_ref, other_ref, rest, labels, start, left, right, spares, main, over, sems):
    groups, all_pairs, _ = rest.shape
    per_quarter = groups // QUARTERS
    split, cut = groups // 2, per_quarter // 2
    half = pl.ds(0, LANES)
    first = [
        pltpu.make_async_copy(rest_hbm, rest, sems.at[0]),
        pltpu.make_async_copy(labels_hbm, labels, sems.at[1]),
    ]
    second = [
        pltpu.make_async_copy(
            low_hbm.at[pl.ds(0, split)], right.at[pl.ds(0, split), :, half], sems.at[2]
        ),
        pltpu.make_async_copy(
            high_hbm.at[pl.ds(0, split)], right.at[pl.ds(split, split), :, half], sems.at[3]
        ),
        pltpu.make_async_copy(low_hbm.at[pl.ds(split, cut)], spares.at[pl.ds(0, cut)], sems.at[4]),
        pltpu.make_async_copy(
            high_hbm.at[pl.ds(split, per_quarter - cut)],
            spares.at[pl.ds(cut, per_quarter - cut)],
            sems.at[5],
        ),
    ]
    third = pltpu.make_async_copy(start_hbm, start, sems.at[6])
    for copy in first + second + [third]:
        copy.start()
    for copy in first:
        copy.wait()
    quarter = iota((1, LANES), 1) // SPARE
    for c in range(groups):
        row = c * slots + slots - 1
        masked_rows(left, c * LANES, rest[c], labels[row : row + 1, :])
    for copy in second:
        copy.wait()
    for c in range(groups):
        right[c, :, LANES:] = spares[c % per_quarter] * one_hot(quarter == c // per_quarter)
    block = right[...].reshape(groups * LANES, 2 * LANES)
    third.wait()
    chunk = 2 * all_pairs
    for m in range(0, left.shape[0], chunk):
        at = slice(m, m + chunk)
        total = start[at] + dot(left[at], block)
        main[at] = total[:, :LANES]
        spare = total[:, LANES:]
        spare = spare + pltpu.roll(spare, 2 * SPARE, 1)
        over[at] = spare + pltpu.roll(spare, SPARE, 1)
    owners = all_pairs // pairs
    lines = mine_ref.shape[0] // (owners // cores)
    run = 8
    per = IRREPS // QUARTERS

    def emit(core, ref):
        ref[...] = jnp.zeros_like(ref)
        for block in range(owners // cores // run):
            owner = (block * cores + core) * run
            base = block * run * lines
            for g in range(IRREPS):
                for p in range(pairs):
                    at = g * all_pairs + owner * pairs + p
                    ref[pl.ds(base + g * pairs + p, run, stride=lines), :] = main[
                        pl.ds(at, run, stride=pairs), :
                    ]
            for g in range(per):
                for p in range(pairs):
                    value = jnp.zeros((run, LANES), jnp.float32)
                    for q in range(QUARTERS):
                        at = (q * per + g) * all_pairs + owner * pairs + p
                        piece = over[pl.ds(at, run, stride=pairs), :]
                        value = value + jnp.where(quarter == q, piece, 0.0)
                    at = base + (IRREPS + g) * pairs + p
                    ref[pl.ds(at, run, stride=lines), :] = value

    for core in range(cores):

        @pl.when(core_ref[0] == core)
        def _():
            emit(core, mine_ref)

        @pl.when(core_ref[0] != core)
        def _():
            emit(core, other_ref)


def contract_last(core, rest, labels, start, low, high, pairs):
    groups, all_pairs, _ = rest.shape
    cores = 2
    owners = all_pairs // pairs
    lines = -(-(IRREPS + IRREPS // QUARTERS) * pairs // 8) * 8
    whole = pl.BlockSpec(memory_space=pltpu.VMEM)
    hbm = pl.BlockSpec(memory_space=pl.ANY)
    tall = IRREPS * all_pairs
    shape = jax.ShapeDtypeStruct((owners // cores * lines, LANES), jnp.float32)
    return pl.pallas_call(
        functools.partial(last_kernel, pairs, labels.shape[0] // groups, cores),
        in_specs=[pl.BlockSpec(memory_space=pltpu.SMEM)] + [hbm] * 5,
        out_specs=[whole, whole],
        out_shape=[shape, shape],
        scratch_shapes=[
            pltpu.VMEM(rest.shape, rest.dtype),
            pltpu.VMEM(labels.shape, labels.dtype),
            pltpu.VMEM(start.shape, start.dtype),
            pltpu.VMEM((tall, groups * LANES), jnp.bfloat16),
            pltpu.VMEM((groups, LANES, 2 * LANES), jnp.bfloat16),
            pltpu.VMEM((groups // QUARTERS, LANES, LANES), jnp.bfloat16),
            pltpu.VMEM((tall, LANES), jnp.float32),
            pltpu.VMEM((tall, LANES), jnp.float32),
            pltpu.SemaphoreType.DMA((7,)),
        ],
        compiler_params=pltpu.CompilerParams(vmem_limit_bytes=18 * MIB),
        cost_estimate=pl.CostEstimate(
            flops=2 * 768 * 2560 * 256, bytes_accessed=3_000_000, transcendentals=0
        ),
        name="contract_last",
    )(core, rest, labels, start, low, high)


def unpack_kernel(pairs, round_ref, parts_ref, rank_ref, slab_ref, rest_ref, out_ref):
    rows = parts_ref.shape[1]
    slab = slab_ref.shape[1]
    summed = parts_ref[0]
    for k in range(1, parts_ref.shape[0]):
        summed = summed + parts_ref[k]
    irrep = slab_ref[...]
    rank = rank_ref[...] - round_ref[0] * CAP
    each = IRREPS // QUARTERS
    inside = (rank >= 0) & (rank < CAP)
    spare = rank >= LANES
    target = jnp.where(spare, (irrep // each) * SPARE + rank - LANES, rank)
    target = jnp.where(inside, target, -1)
    pick = jnp.where(iota((LANES, slab), 0) == target, 1.0, 0.0)
    values = jnp.dot(
        summed, pick, preferred_element_type=jnp.float32, precision=lax.Precision.HIGHEST
    )
    first = jnp.where(spare, (IRREPS + irrep % each) * pairs, irrep * pairs)
    row = iota((rows, slab), 0)
    for p in range(pairs):
        out_ref[p : p + 1, :] = rest_ref[p : p + 1, :] + jnp.sum(
            jnp.where(row == first + p, values, 0.0), axis=0, keepdims=True
        )


def unpack(which, parts, rank, slab_irrep, rest):
    pairs, slab = rest.shape
    whole = pl.BlockSpec(memory_space=pltpu.VMEM)
    return pl.pallas_call(
        functools.partial(unpack_kernel, pairs),
        in_specs=[pl.BlockSpec(memory_space=pltpu.SMEM), whole, whole, whole, whole],
        out_specs=whole,
        out_shape=jax.ShapeDtypeStruct((pairs, slab), jnp.float32),
        compiler_params=pltpu.CompilerParams(vmem_limit_bytes=6 * MIB),
        name="unpack",
    )(which, parts, rank, slab_irrep.reshape(1, slab), rest)


def local(amplitudes, integrals, virt_irrep, slab_irrep):
    pairs = amplitudes.shape[0]
    owners = lax.axis_size("va")
    count = lax.axis_size("vb")
    parts = lax.axis_size("occ")
    first_width, second_width, _ = integrals.shape
    folds = LANES // second_width
    groups = first_width // folds
    here = lax.axis_index("vb")
    part = lax.axis_index("occ")

    first_labels = lax.dynamic_slice_in_dim(
        virt_irrep, lax.axis_index("va") * first_width, first_width, 0
    )
    second_labels = lax.dynamic_index_in_dim(
        virt_irrep.reshape(count, parts, second_width), part, 1, keepdims=False
    )
    own_labels = lax.dynamic_index_in_dim(second_labels, here, 0, keepdims=False)
    order = lax.rem(here + jnp.array(AWAYS, jnp.int32), count)
    labels = jnp.bitwise_xor(
        first_labels.reshape(groups, 1, folds, 1),
        jnp.take(second_labels, order, axis=0).reshape(1, count, 1, second_width),
    ).reshape(groups, count, folds * second_width)
    labels = jnp.pad(
        labels, ((0, 0), (0, 0), (0, LANES - folds * second_width)), constant_values=-1
    )
    near_labels = labels[:, : count // 2].reshape(-1, LANES)
    far_labels = labels[:, count // 2 :].reshape(-1, LANES)

    up = [(i, (i + 1) % count) for i in range(count)]
    down = [(i, (i - 1) % count) for i in range(count)]

    same_core = [
        [(2 * k + core) * owners + i for k in range(parts // 2) for i in range(owners)]
        for core in range(2)
    ]

    def shifted(pair, perm):
        return tuple(lax.ppermute(block, "vb", perm) for block in pair)

    def blocks_of(which, after):
        low, high, rank = pack_integrals(
            which, integrals, first_labels, own_labels, slab_irrep, after
        )
        packed = low, high
        r1, l1 = shifted(packed, up), shifted(packed, down)
        r2, l2 = shifted(r1, up), shifted(l1, down)
        r3, l3 = shifted(r2, up), shifted(l2, down)
        return (packed, l1, r1, l2), (r2, r3, l3), rank

    def finish(which, near, middle, rank, arrived, rest_of_sum):
        (start,) = contract(arrived, near_labels, None, near, 0)
        up_end, down_end, start = lax.optimization_barrier((middle[1][0], middle[2][1], start))
        far = lax.ppermute(up_end, "vb", up), lax.ppermute(down_end, "vb", down)
        start, rest = contract(arrived, far_labels, start, middle, 1)
        core = lax.rem(part, 2)
        mine, other = contract_last(core.reshape(1), rest, far_labels, start, *far, pairs)
        partial = mine + lax.ppermute(other, "occ", [(i, i ^ 1) for i in range(parts)])
        partial = partial.reshape(parts // 2 * owners, -1, LANES)
        summands = lax.all_to_all(
            partial, SOURCES, split_axis=0, concat_axis=0, tiled=True, axis_index_groups=same_core
        )
        return unpack(which, summands, rank, slab_irrep, rest_of_sum)

    first = jnp.zeros((1,), jnp.int32)
    spread = spread_amplitudes(here.reshape(1), amplitudes, owners, count, parts)
    sent = spread.reshape((parts * owners,) + spread.shape[2:])
    arrived = lax.all_to_all(sent, SOURCES, split_axis=0, concat_axis=0, tiled=True)
    arrived = arrived.reshape((parts * owners * pairs,) + spread.shape[3:])
    near, middle, rank = blocks_of(first, spread)
    largest = jnp.max(rank)

    def more(carry):
        return carry[0] * CAP <= largest

    def step(carry):
        which = carry[0].reshape(1)
        near, middle, rank = blocks_of(which, spread)
        return carry[0] + 1, finish(which, near, middle, rank, arrived, carry[1])

    nothing = jnp.zeros((pairs, slab_irrep.shape[0]), jnp.float32)
    later = lax.while_loop(more, step, (jnp.int32(1), nothing))[1]
    return finish(first, near, middle, rank, arrived, later)


def solution(mesh):
    return jax.shard_map(
        local,
        mesh=mesh,
        in_specs=(P(("va", "vb", "occ"), None, None), P("va", ("vb", "occ"), None), P(), P()),
        out_specs=P(("va", "vb", "occ"), None),
        check_vma=False,
    )
```
